256 devices in a mesh: gx: 16 (over y_lo, x, core), gy: 16 (over y_hi, z).
Axes of the slice: x: 4, y: 4 (y_hi: 2, y_lo: 2; y = y_hi * 2 + y_lo), z: 8, core: 2. Of those that a mesh axis runs over, the one named last changes fastest.
Arguments:
- model_one: float32 [8, 256, 2048], P(None, 'gx', 'gy'), may hold values from -6 to 6
- model_two: float32 [8, 256, 2048], P(None, 'gx', 'gy'), may hold values from -6 to 6
- coupling_weight: float32 [8, 256, 2048], P(None, 'gx', 'gy'), may hold values from 0.2 to 2
- direction_one: float32 [10, 8, 256, 2048], P(None, None, 'gx', 'gy'), may hold values from -6 to 6
- direction_two: float32 [10, 8, 256, 2048], P(None, None, 'gx', 'gy'), may hold values from -6 to 6
Outputs:
- grad_one: float32 [8, 256, 2048], P(None, 'gx', 'gy')
- grad_two: float32 [8, 256, 2048], P(None, 'gx', 'gy')
- hess_one: float32 [10, 8, 256, 2048], P(None, None, 'gx', 'gy')
- hess_two: float32 [10, 8, 256, 2048], P(None, None, 'gx', 'gy')
The draws below stay inside these ranges and needn't reach their ends.
All inputs are finite; a program needn't handle non-finite values.
Results may differ from the reference program's by a relative error of at most 0.00013.
Values sent between devices are 32-bit elements; how exact they have to be, the bound alone decides.
No kernel may reach another device: no remote copies, remote signals or barrier semaphores. Data moves between devices by JAX's collectives and lax.ppermute only.
A program may use at most 64 MiB of HBM per device.

```python
import math
import jax
import jax.numpy as jnp
from jax import lax

NZ = 8
DIRS = 10
NX = 256
NY = 2048


def shard_levels(stream_key, dims, pieces, smallest, largest):
    gain = 1.0
    for axis_at, parts in pieces:
        heights = jax.random.uniform(jax.random.fold_in(jax.random.fold_in(stream_key, 6), axis_at), (parts,), jnp.float32, smallest / len(pieces), largest / len(pieces))
        gain = gain * jnp.repeat(jnp.exp(heights), dims[axis_at] // parts).reshape((-1,) + (1,) * (len(dims) - 1 - axis_at))
    return gain


def scatter_about(key, extent, scale, bound, cuts=(), kind=jnp.bfloat16):
    entries = jax.random.normal(key, extent, jnp.float32) * scale
    if len(cuts) > 0:
        entries = shard_levels(key, extent, cuts, -0.22, 0.18) * entries
    return jnp.clip(entries, min=-bound, max=bound).astype(kind)


def setup_inputs(seed: int = 0) -> dict:
    seeds = jax.random.split(jax.random.key(seed), 6)
    return {
        "model_one": scatter_about(seeds[0], (NZ, NX, NY), 1.0, 6.0, ((1, 16), (2, 16)), jnp.float32),
        "model_two": scatter_about(seeds[1], (NZ, NX, NY), 1.0, 6.0, ((1, 16), (2, 16)), jnp.float32),
        "coupling_weight": jnp.clip(jnp.exp(math.log(2.0) - 2.3025851 * jax.random.uniform(seeds[2], (NZ, NX, NY), jnp.float32) ** shard_levels(seeds[2], (NZ, NX, NY), ((1, 16), (2, 16)), -0.2, 0.2)), 0.2, 2.0),
        "direction_one": scatter_about(seeds[3], (DIRS, NZ, NX, NY), 1.0, 6.0, ((2, 16), (3, 16)), jnp.float32),
        "direction_two": scatter_about(seeds[4], (DIRS, NZ, NX, NY), 1.0, 6.0, ((2, 16), (3, 16)), jnp.float32),
    }


def central(padded, along, length):
    def shifted(offset):
        return lax.slice_in_dim(padded, 2 + offset, 2 + offset + length, axis=along)
    return (8.0 * (shifted(1) - shifted(-1)) - (shifted(2) - shifted(-2))) / 12.0


def padded_along(field, along):
    padding = [(0, 0)] * field.ndim
    padding[along] = (2, 2)
    return jnp.pad(field, padding)


def gradient3(field):
    base = field.ndim
    return tuple(central(padded_along(field, base + neg), base + neg, field.shape[base + neg]) for neg in (-2, -1, -3))


def divergence(vector):
    base = vector[0].ndim
    total = jnp.zeros(vector[0].shape, jnp.float32)
    for component, neg in zip(vector, (-2, -1, -3)):
        total = total + central(padded_along(component, base + neg), base + neg, component.shape[base + neg])
    return -total


def cross_product(left, right):
    return (left[1] * right[2] - left[2] * right[1],
            left[2] * right[0] - left[0] * right[2],
            left[0] * right[1] - left[1] * right[0])


def reference(model_one, model_two, coupling_weight, direction_one, direction_two):
    slope_one = gradient3(model_one)
    slope_two = gradient3(model_two)
    coupled = cross_product(slope_one, slope_two)
    weighted = tuple(coupling_weight * part for part in coupled)
    grad_one = divergence(cross_product(slope_two, weighted))
    grad_two = divergence(cross_product(weighted, slope_one))

    def one_pair(pair):
        first, second = pair
        left_term = cross_product(gradient3(first), slope_two)
        right_term = cross_product(slope_one, gradient3(second))
        reweighted = tuple(coupling_weight * (left_term[index] + right_term[index]) for index in range(3))
        return divergence(cross_product(slope_two, reweighted)), divergence(cross_product(reweighted, slope_one))

    hess_one, hess_two = lax.map(one_pair, (direction_one, direction_two))
    return grad_one, grad_two, hess_one, hess_two
```

```python
import functools

import jax
import jax.numpy as jnp
from jax import lax
from jax.experimental import pallas as pl
from jax.experimental.pallas import tpu as pltpu
from jax.sharding import PartitionSpec as P

LAYERS = 8
ROWS = 16
EXT = 24
LANES = 128
MIB = 1024 * 1024
F32 = jnp.float32


def swap(count, first):
    pairs = []
    for low in range(first, count - 1, 2):
        pairs += [(low, low + 1), (low + 1, low)]
    return pairs


def shape(*dims):
    return jax.ShapeDtypeStruct(dims, F32)


def lane(dims):
    return lax.broadcasted_iota(jnp.int32, dims, len(dims) - 1)


def sub(dims):
    return lax.broadcasted_iota(jnp.int32, dims, len(dims) - 2)


def lroll(value, amount):
    return pltpu.roll(value, amount % LANES, axis=value.ndim - 1)


def sroll(value, amount):
    return pltpu.roll(value, amount % value.shape[-2], axis=value.ndim - 2)


def pack_body(dirs, m1, m2, w, d1, d2, xs, xb, xa, e1, e2):
    core = lax.rem(lax.axis_index("gx"), 2)
    tile = (8, LANES)
    upper = (sub(tile) >= 4).astype(jnp.int32)

    def edge_rows(one, two, tail, layer):
        start = pl.multiple_of(tail * 8, 8)
        first = one[layer, pl.ds(start, 8), :]
        second = two[layer, pl.ds(start, 8), :]
        return jnp.where(upper == tail, first, sroll(second, 4))

    a_tail = 1 - core
    b_tail = core

    def rows(index, one, two):
        for layer in range(LAYERS):
            xb[index, layer] = edge_rows(one, two, b_tail, layer)
            xa[index, layer] = edge_rows(one, two, a_tail, layer)

    block = lane((ROWS, LANES)) // 8
    for layer in range(LAYERS):
        first = jnp.zeros((ROWS, LANES), F32)
        second = jnp.zeros((ROWS, LANES), F32)
        for d in range(dirs):
            first = jnp.where(block == d, lroll(d1[d, layer], 8 * d + 4), first)
            second = jnp.where(block == d, lroll(d2[d, layer], 8 * d + 4), second)
        first = jnp.where(block == dirs, lroll(m1[layer], 8 * dirs + 4), first)
        first = jnp.where(block == dirs + 1, lroll(w[layer], 8 * dirs + 12), first)
        second = jnp.where(block == dirs + 1, lroll(m2[layer], 8 * dirs + 12), second)
        e1[layer] = first
        e2[layer] = second
    for layer in range(LAYERS):
        xs[layer] = edge_rows(e1, e2, b_tail, layer)
        xa[dirs + 2, layer] = edge_rows(e1, e2, a_tail, layer)

    @pl.loop(0, dirs)
    def _(d):
        rows(d, d1.at[d], d2.at[d])

    rows(dirs, m1, m2)
    rows(dirs + 1, w, w)


def join_rows(core, from_a, from_b):
    mask = ((sub(from_a.shape) < 4).astype(jnp.int32) + core) == 1
    return jnp.where(mask, from_a, from_b), sroll(jnp.where(mask, from_b, from_a), 4)


def edges_body(e1, e2, xa, xs, e1x, e2x, ya, yb):
    core = lax.rem(lax.axis_index("gx"), 2)
    side = lax.rem(lax.axis_index("gy"), 2)
    for layer in range(LAYERS):
        one, two = join_rows(core, xa[layer], xs[layer])
        one = jnp.concatenate([e1[layer], one], 0)
        two = jnp.concatenate([e2[layer], two], 0)
        e1x[layer] = one
        e2x[layer] = two
        low = (lane(one.shape) % 8) < 4
        tail = jnp.where(low, one, lroll(two, 4))
        head = jnp.where(low, lroll(two, -4), one)
        ya[layer] = jnp.where(side == 0, tail, head)
        yb[layer] = jnp.where(side == 0, head, tail)


def stencil(up2, up1, down1, down2):
    return 8.0 * (up1 - down1) - (up2 - down2)


def diff_x(value):
    return stencil(sroll(value, -2), sroll(value, -1), sroll(value, 1), sroll(value, 2))


def diff_y(value):
    return stencil(lroll(value, -2), lroll(value, -1), lroll(value, 1), lroll(value, 2))


def diff_z(ref, layer, rows=None):
    def at(offset):
        where = layer + offset
        if where < 0 or where >= LAYERS:
            return None
        return ref[where] if rows is None else ref[where, rows, :]

    total = None
    for offset, factor in ((1, 8.0), (-1, -8.0), (2, -1.0), (-2, 1.0)):
        part = at(offset)
        if part is None:
            continue
        if total is None:
            total = factor * part if factor != 1.0 else part
        elif factor == -1.0:
            total = total - part
        elif factor == 1.0:
            total = total + part
        elif at(-offset) is not None and offset == -1:
            total = 8.0 * (at(1) - part)
        else:
            total = total + factor * part
    return total


def cross(left, right):
    return (
        left[1] * right[2] - left[2] * right[1],
        left[2] * right[0] - left[0] * right[2],
        left[0] * right[1] - left[1] * right[0],
    )


def field_body(
    dirs, m1, m2, w, d1, d2, xa, xb, e1x, e2x, ya, yb,
    g1, g2, h1, h2,
    f_ext, g_ext, w_ext, s1, s2, dy1, dy2, hy1, hy2, hx, hz1, hz2, hsrc1, hsrc2, cor1, cor2, ax, ay, az,
):
    core = lax.rem(lax.axis_index("gx"), 2)
    side = lax.rem(lax.axis_index("gy"), 2)
    full = (EXT, LANES)
    lanes = lane(full)
    low = (lanes % 8) < 4
    edge = (lanes < 2) | (lanes >= 126)

    def load_ext(one, two, message, layer):
        tail1, tail2 = join_rows(core, xa[message, layer], xb[message, layer])
        f_ext[layer] = jnp.concatenate([one[layer], tail1], 0)
        g_ext[layer] = jnp.concatenate([two[layer], tail2], 0)

    for layer in range(LAYERS):
        from_a, from_b = ya[layer], yb[layer]
        left = jnp.where(side == 0, from_b, from_a)
        right = jnp.where(side == 0, from_a, from_b)
        left2, right2 = lroll(left, -4), lroll(right, 4)
        for src, left_i, right_i, halo, dy, hy in (
            (e1x, left, right, hsrc1, dy1, hy1),
            (e2x, left2, right2, hsrc2, dy2, hy2),
        ):
            own = src[layer]
            before = diff_y(jnp.where(low, left_i, own))
            after = diff_y(jnp.where(low, own, right_i))
            halo[layer] = jnp.where(low, left_i, right_i)
            dy[layer] = jnp.where(low, after, before)
            hy[layer] = jnp.where(low, before, after)

    fold = -1.0 / 20736.0
    for layer in range(LAYERS):
        load_ext(m1, m2, dirs, layer)
        wt, _ = join_rows(core, xa[dirs + 1, layer], xb[dirs + 1, layer])
        w_ext[layer] = jnp.concatenate([w[layer], wt], 0) * fold

    def slopes(ext, dy, amount, layer):
        value = ext[layer]
        slope_y = jnp.where(edge, pltpu.roll(dy[layer], amount, axis=1), diff_y(value))
        return diff_x(value), slope_y, diff_z(ext, layer)

    for layer in range(LAYERS):
        for ref, ext, dy, at in ((s1, f_ext, dy1, dirs), (s2, g_ext, dy2, dirs + 1)):
            for index, part in enumerate(slopes(ext, dy, (124 - 8 * at) % LANES, layer)):
                ref[index, layer] = part

    main = pl.ds(0, ROWS)
    block = lane((ROWS, LANES)) // 8
    kind = lane((ROWS, LANES)) % 8

    def spread(value, at):
        value = jnp.where(block == at, value, 0.0)
        for amount in (8, 16, 32, 64):
            value = value + lroll(value, amount)
        return value

    for layer in range(LAYERS):
        first = (diff_x(hsrc1[layer])[:ROWS], hy1[layer, main, :], diff_z(hsrc1, layer, main))
        second = (diff_x(hsrc2[layer])[:ROWS], hy2[layer, main, :], diff_z(hsrc2, layer, main))
        one = tuple(spread(part, dirs) for part in first)
        two = tuple(spread(part, dirs + 1) for part in second)
        weight = spread(hsrc1[layer, main, :], dirs + 1) * fold
        second = tuple(jnp.where(block == dirs, 0.0, part) for part in second)
        left_term = cross(first, two)
        right_term = cross(one, second)
        rw = tuple(weight * (left_term[i] + right_term[i]) for i in range(3))
        for value, cor in ((cross(two, rw)[1], cor1), (cross(rw, one)[1], cor2)):
            value_up1, value_up2 = lroll(value, -1), lroll(value, -2)
            value_down1, value_down2 = lroll(value, 1), lroll(value, 2)
            cor[layer] = jnp.where(
                kind == 2,
                -value_up2,
                jnp.where(
                    kind == 3,
                    8.0 * value_up1 - value_up2,
                    jnp.where(kind == 4, value_down2 - 8.0 * value_down1, value_down2),
                ),
            )

    lanes16 = lane((ROWS, LANES))
    edge16 = (lanes16 < 2) | (lanes16 >= 126)
    up1 = jnp.where(lanes16 < 127, 8.0, 0.0)
    down1 = jnp.where(lanes16 >= 1, 8.0, 0.0)
    up2 = jnp.where(lanes16 < 126, 1.0, 0.0)
    down2 = jnp.where(lanes16 >= 2, 1.0, 0.0)

    def pair(amount, outs, second_field):
        for layer in range(LAYERS):
            one = (s1[0, layer], s1[1, layer], s1[2, layer])
            two = (s2[0, layer], s2[1, layer], s2[2, layer])
            if second_field:
                perturbed = tuple(
                    p + q
                    for p, q in zip(
                        cross(slopes(f_ext, dy1, amount, layer), two), cross(one, slopes(g_ext, dy2, amount, layer))
                    )
                )
            else:
                perturbed = cross(one, two)
            weight = w_ext[layer]
            rw = tuple(weight * part for part in perturbed)
            for k, adj in ((0, cross(two, rw)), (1, cross(rw, one))):
                ax[k, layer] = adj[0]
                ay[k, layer] = adj[1][:ROWS]
                az[k, layer] = adj[2][:ROWS]
        for k, cor in ((0, cor1), (1, cor2)):
            for layer in range(LAYERS):
                y = ay[k, layer]
                part_y = (up1 * lroll(y, -1) - down1 * lroll(y, 1)) - (up2 * lroll(y, -2) - down2 * lroll(y, 2))
                part_y = part_y + jnp.where(edge16, pltpu.roll(cor[layer], amount, axis=1), 0.0)
                outs[k][layer] = diff_x(ax[k, layer])[:ROWS] + part_y + diff_z(az.at[k], layer)

    pair((124 - 8 * dirs) % LANES, (g1, g2), False)

    @pl.loop(0, dirs)
    def _(d):
        for layer in range(LAYERS):
            load_ext(d1.at[d], d2.at[d], d, layer)
        pair(124 - 8 * d, (h1.at[d], h2.at[d]), True)


def params():
    return pltpu.CompilerParams(vmem_limit_bytes=40 * MIB)


def shards(model_one, model_two, weight, direction_one, direction_two):
    dirs = direction_one.shape[0]
    tile = shape(LAYERS, ROWS, LANES)
    ext = shape(LAYERS, EXT, LANES)
    small = shape(LAYERS, 8, LANES)
    fields = (model_one, model_two, weight, direction_one, direction_two)
    xs, xb, xa, e1, e2 = pl.pallas_call(
        functools.partial(pack_body, dirs),
        out_shape=(small, shape(dirs + 2, LAYERS, 8, LANES), shape(dirs + 3, LAYERS, 8, LANES), tile, tile),
        compiler_params=params(),
        name="pack",
    )(*fields)
    count_x, count_y = lax.axis_size("gx"), lax.axis_size("gy")
    xs = lax.ppermute(xs, "gx", swap(count_x, 1))
    xb = lax.ppermute(xb, "gx", swap(count_x, 1))
    xa = lax.ppermute(xa, "gx", swap(count_x, 0))
    e1x, e2x, ya, yb = pl.pallas_call(
        edges_body,
        out_shape=(ext,) * 4,
        compiler_params=params(),
        name="edges",
    )(e1, e2, xa[dirs + 2], xs)
    yb = lax.ppermute(yb, "gy", swap(count_y, 1))
    ya = lax.ppermute(ya, "gy", swap(count_y, 0))
    scratch = lambda *dims: pltpu.VMEM(dims, F32)
    many = shape(dirs, LAYERS, ROWS, LANES)
    ext_s = scratch(LAYERS, EXT, LANES)
    ext_3 = scratch(3, LAYERS, EXT, LANES)
    tile_s = scratch(LAYERS, ROWS, LANES)
    tile_2 = scratch(2, LAYERS, ROWS, LANES)
    return pl.pallas_call(
        functools.partial(field_body, dirs),
        out_shape=(tile, tile, many, many),
        scratch_shapes=[
            ext_s, ext_s, ext_s, ext_3, ext_3, ext_s, ext_s, ext_s, ext_s, ext_s, ext_s, ext_s, ext_s, ext_s,
            tile_s, tile_s, scratch(2, LAYERS, EXT, LANES), tile_2, tile_2,
        ],
        compiler_params=params(),
        name="fields",
    )(*fields, xa, xb, e1x, e2x, ya, yb)


def solution(mesh):
    plane = P(None, "gx", "gy")
    stack = P(None, None, "gx", "gy")
    return jax.shard_map(
        shards,
        mesh=mesh,
        in_specs=(plane, plane, plane, stack, stack),
        out_specs=(plane, plane, stack, stack),
        check_vma=False,
    )
```

```python
import functools

import jax
import jax.numpy as jnp
from jax import lax
from jax.experimental import pallas as pl
from jax.experimental.pallas import tpu as pltpu
from jax.sharding import PartitionSpec as P

LAYERS = 8
ROWS = 16
EXT = 24
LANES = 128
MIB = 1024 * 1024
F32 = jnp.float32


def swap(count, first):
    pairs = []
    for low in range(first, count - 1, 2):
        pairs += [(low, low + 1), (low + 1, low)]
    return pairs


def shape(*dims):
    return jax.ShapeDtypeStruct(dims, F32)


def scratch(*dims):
    return pltpu.VMEM(dims, F32)


def half(*dims):
    return pltpu.VMEM(dims, jnp.bfloat16)


def lane(dims):
    return lax.broadcasted_iota(jnp.int32, dims, len(dims) - 1)


def sub(dims):
    return lax.broadcasted_iota(jnp.int32, dims, len(dims) - 2)


def lroll(value, amount):
    return pltpu.roll(value, amount % LANES, axis=value.ndim - 1)


def sroll(value, amount):
    return pltpu.roll(value, amount % value.shape[-2], axis=value.ndim - 2)


def edge_rows(one, two, tail, layer):
    upper = (sub((8, LANES)) >= 4).astype(jnp.int32)
    start = pl.multiple_of(tail * 8, 8)
    first = one[layer, pl.ds(start, 8), :]
    second = two[layer, pl.ds(start, 8), :]
    return jnp.where(upper == tail, first, sroll(second, 4))


def message_rows(dirs, tail, out, m1, m2, w, d1, d2):
    def rows(index, one, two):
        for layer in range(LAYERS):
            out[index, layer] = edge_rows(one, two, tail, layer)

    for d in range(dirs):
        rows(d, d1.at[d], d2.at[d])
    rows(dirs, m1, m2)
    rows(dirs + 1, w, w)


def far_body(dirs, first, m1, m2, w, d1, d2, xb):
    message_rows(dirs, lax.rem(lax.axis_index("gx"), 2), xb, m1, m2, w, d1, d2)


def pack_body(dirs, first, m1, m2, w, d1, d2, xs, xa, e1, e2):
    core = lax.rem(lax.axis_index("gx"), 2)
    a_tail = 1 - core
    b_tail = core

    block = lane((ROWS, LANES)) // 8
    for layer in range(LAYERS):
        first = jnp.zeros((ROWS, LANES), F32)
        second = jnp.zeros((ROWS, LANES), F32)
        for d in range(dirs):
            first = jnp.where(block == d, lroll(d1[d, layer], 8 * d + 4), first)
            second = jnp.where(block == d, lroll(d2[d, layer], 8 * d + 4), second)
        first = jnp.where(block == dirs, lroll(m1[layer], 8 * dirs + 4), first)
        first = jnp.where(block == dirs + 1, lroll(w[layer], 8 * dirs + 12), first)
        second = jnp.where(block == dirs + 1, lroll(m2[layer], 8 * dirs + 12), second)
        e1[layer] = first
        e2[layer] = second
    for layer in range(LAYERS):
        xs[layer] = edge_rows(e1, e2, b_tail, layer)
        xa[dirs + 2, layer] = edge_rows(e1, e2, a_tail, layer)

    message_rows(dirs, a_tail, xa, m1, m2, w, d1, d2)


def join_rows(core, from_a, from_b):
    mask = ((sub(from_a.shape) < 4).astype(jnp.int32) + core) == 1
    return jnp.where(mask, from_a, from_b), sroll(jnp.where(mask, from_b, from_a), 4)


def edges_body(e1, e2, xa, xs, e1x, e2x, ya, yb):
    core = lax.rem(lax.axis_index("gx"), 2)
    side = lax.rem(lax.axis_index("gy"), 2)
    for layer in range(LAYERS):
        one, two = join_rows(core, xa[layer], xs[layer])
        one = jnp.concatenate([e1[layer], one], 0)
        two = jnp.concatenate([e2[layer], two], 0)
        e1x[layer] = one
        e2x[layer] = two
        low = (lane(one.shape) % 8) < 4
        tail = jnp.where(low, one, lroll(two, 4))
        head = jnp.where(low, lroll(two, -4), one)
        ya[layer] = jnp.where(side == 0, tail, head)
        yb[layer] = jnp.where(side == 0, head, tail)


def stencil(up2, up1, down1, down2):
    return 8.0 * (up1 - down1) - (up2 - down2)


def diff_x(value):
    return stencil(sroll(value, -2), sroll(value, -1), sroll(value, 1), sroll(value, 2))


def diff_y(value):
    return stencil(lroll(value, -2), lroll(value, -1), lroll(value, 1), lroll(value, 2))


def diff_z(ref, layer, rows=None):
    def at(offset):
        where = layer + offset
        if where < 0 or where >= LAYERS:
            return None
        return ref[where] if rows is None else ref[where, rows, :]

    total = None
    for offset, factor in ((1, 8.0), (-1, -8.0), (2, -1.0), (-2, 1.0)):
        part = at(offset)
        if part is None:
            continue
        if total is None:
            total = factor * part if factor != 1.0 else part
        elif factor == -1.0:
            total = total - part
        elif factor == 1.0:
            total = total + part
        elif at(-offset) is not None and offset == -1:
            total = 8.0 * (at(1) - part)
        else:
            total = total + factor * part
    return total


def cross(left, right):
    return (
        left[1] * right[2] - left[2] * right[1],
        left[2] * right[0] - left[0] * right[2],
        left[0] * right[1] - left[1] * right[0],
    )


def split3(value):
    high = value.astype(jnp.bfloat16)
    rest = value - high.astype(F32)
    mid = rest.astype(jnp.bfloat16)
    return high, mid, (rest - mid.astype(F32)).astype(jnp.bfloat16)


def band():
    gap = lax.broadcasted_iota(jnp.int32, (LANES, LANES), 0) - lax.broadcasted_iota(jnp.int32, (LANES, LANES), 1)
    near = jnp.where(gap == 1, 8.0, jnp.where(gap == -1, -8.0, 0.0))
    far = jnp.where(gap == 2, -1.0, jnp.where(gap == -2, 1.0, 0.0))
    return (near + far).astype(jnp.bfloat16)


def edge_rows_matrix(block):
    row = lax.broadcasted_iota(jnp.int32, (16, LANES), 0) - 8 * (block % 2)
    col = lax.broadcasted_iota(jnp.int32, (16, LANES), 1)
    table = jnp.zeros((16, LANES), F32)
    for k, c, factor in ((2, 0, 1.0), (3, 0, -8.0), (3, 1, 1.0), (4, 126, -1.0), (4, 127, 8.0), (5, 127, -1.0)):
        table = jnp.where((row == k) & (col == c), factor, table)
    return table.astype(jnp.bfloat16)


def setup_body(mats):
    mats[...] = jnp.zeros(mats.shape, jnp.bfloat16)
    for block in range(mats.shape[0]):
        mats[block, :LANES, :] = band()
        start = LANES + 16 * (block // 2)
        mats[block, start : start + 16, :] = edge_rows_matrix(block)


def field_body(
    dirs, mats, m1, m2, w, d1, d2, xa, xb, e1x, e2x, ya, yb,
    g1_out, g2_out, h1_out, h2_out,
    g1, g2, h1, h2, out_sems,
    ext_refs, w_ext, s1, s2, hy1, hy2, hsrc1, hsrc2, cor1, cor2, ax, ay, az, lhs_f, lhs_a, res_f, res_a,
):
    core = lax.rem(lax.axis_index("gx"), 2)
    side = lax.rem(lax.axis_index("gy"), 2)
    full = (EXT, LANES)
    low = (lane(full) % 8) < 4
    flat = (LAYERS * EXT, LANES)
    flat16 = (LAYERS * ROWS, LANES)

    def put(lhs, index, value, right=False):
        rows = value.shape[0]
        for part, at in zip(split3(value), range(3)):
            start = (3 * index + at) * rows
            if right:
                lhs[start : start + rows, LANES:] = part
            else:
                lhs[start : start + rows, :LANES] = part

    def multiply(lhs, result, block):
        result[...] = jnp.dot(lhs[...], mats[block], preferred_element_type=F32)

    def column(result, rows, index, layer):
        per = result.shape[0] // 6
        start = 3 * index * per + layer * rows
        return (result[start : start + rows] + result[start + per : start + per + rows]) + result[
            start + 2 * per : start + 2 * per + rows
        ]

    def load_ext(slot, one, two, message):
        for layer in range(LAYERS):
            tail1, tail2 = join_rows(core, xa[message, layer], xb[message, layer])
            ext_refs[slot, 0, layer] = jnp.concatenate([one[layer], tail1], 0)
            ext_refs[slot, 1, layer] = jnp.concatenate([two[layer], tail2], 0)
        for index in (0, 1):
            put(lhs_f.at[slot], index, ext_refs[slot, index].reshape(flat))

    for layer in range(LAYERS):
        from_a, from_b = ya[layer], yb[layer]
        left = jnp.where(side == 0, from_b, from_a)
        right = jnp.where(side == 0, from_a, from_b)
        left2, right2 = lroll(left, -4), lroll(right, 4)
        for src, left_i, right_i, halo, hy in ((e1x, left, right, hsrc1, hy1), (e2x, left2, right2, hsrc2, hy2)):
            own = src[layer]
            before = diff_y(jnp.where(low, left_i, own))
            after = diff_y(jnp.where(low, own, right_i))
            halo[layer] = jnp.where(low, left_i, right_i)
            hy[layer] = jnp.where(low, before, after)
    for slot in (0, 1):
        for index, halo in ((0, hsrc1), (1, hsrc2)):
            put(lhs_f.at[slot], index, halo[...].reshape(flat), True)

    fold = -1.0 / 20736.0
    for layer in range(LAYERS):
        wt, _ = join_rows(core, xa[dirs + 1, layer], xb[dirs + 1, layer])
        w_ext[layer] = jnp.concatenate([w[layer], wt], 0) * fold

    def slopes(slot, index, layer):
        ext = ext_refs.at[slot, index]
        return diff_x(ext[layer]), column(res_f.at[slot], EXT, index, layer), diff_z(ext, layer)

    load_ext(0, m1, m2, dirs)
    multiply(lhs_f.at[0], res_f.at[0], dirs)
    multiply(lhs_f.at[0], res_f.at[1], dirs + 1)
    for layer in range(LAYERS):
        for index, ref in ((0, s1), (1, s2)):
            ext = ext_refs.at[0, index]
            ref[0, layer] = diff_x(ext[layer])
            ref[1, layer] = column(res_f.at[index], EXT, index, layer)
            ref[2, layer] = diff_z(ext, layer)

    main = pl.ds(0, ROWS)
    block = lane((ROWS, LANES)) // 8

    def spread(value, at):
        value = jnp.where(block == at, value, 0.0)
        for amount in (8, 16, 32, 64):
            value = value + lroll(value, amount)
        return value

    for layer in range(LAYERS):
        first = (diff_x(hsrc1[layer])[:ROWS], hy1[layer, main, :], diff_z(hsrc1, layer, main))
        second = (diff_x(hsrc2[layer])[:ROWS], hy2[layer, main, :], diff_z(hsrc2, layer, main))
        one = tuple(spread(part, dirs) for part in first)
        two = tuple(spread(part, dirs + 1) for part in second)
        weight = spread(hsrc1[layer, main, :], dirs + 1) * fold
        second = tuple(jnp.where(block == dirs, 0.0, part) for part in second)
        left_term = cross(first, two)
        right_term = cross(one, second)
        rw = tuple(weight * (left_term[i] + right_term[i]) for i in range(3))
        cor1[layer] = cross(two, rw)[1]
        cor2[layer] = cross(rw, one)[1]
    for slot in (0, 1):
        for index, cor in ((0, cor1), (1, cor2)):
            put(lhs_a.at[slot], index, cor[...].reshape(flat16), True)

    def products(slot, second_field):
        for layer in range(LAYERS):
            one = (s1[0, layer], s1[1, layer], s1[2, layer])
            two = (s2[0, layer], s2[1, layer], s2[2, layer])
            if second_field:
                perturbed = tuple(
                    p + q for p, q in zip(cross(slopes(slot, 0, layer), two), cross(one, slopes(slot, 1, layer)))
                )
            else:
                perturbed = cross(one, two)
            weight = w_ext[layer]
            rw = tuple(weight * part for part in perturbed)
            for k, adj in ((0, cross(two, rw)), (1, cross(rw, one))):
                ax[slot, k, layer] = adj[0]
                ay[slot, k, layer] = adj[1][:ROWS]
                az[slot, k, layer] = adj[2][:ROWS]
        for k in (0, 1):
            put(lhs_a.at[slot], k, ay[slot, k].reshape(flat16))

    def divergence(slot, outs):
        for k in (0, 1):
            for layer in range(LAYERS):
                outs[k][layer] = (
                    diff_x(ax[slot, k, layer])[:ROWS]
                    + column(res_a.at[slot], ROWS, k, layer)
                    + diff_z(az.at[slot, k], layer)
                )

    def results(d):
        return (
            pltpu.make_async_copy(h1.at[d], h1_out.at[d], out_sems.at[0, d]),
            pltpu.make_async_copy(h2.at[d], h2_out.at[d], out_sems.at[1, d]),
        )

    products(0, False)
    multiply(lhs_a.at[0], res_a.at[0], dirs)
    divergence(0, (g1, g2))
    last = (
        pltpu.make_async_copy(g1, g1_out, out_sems.at[0, dirs]),
        pltpu.make_async_copy(g2, g2_out, out_sems.at[1, dirs]),
    )
    for copy in last:
        copy.start()

    @pl.loop(0, dirs // 2)
    def _(step):
        d, e = 2 * step, 2 * step + 1
        load_ext(0, d1.at[d], d2.at[d], d)
        multiply(lhs_f.at[0], res_f.at[0], d)
        load_ext(1, d1.at[e], d2.at[e], e)
        multiply(lhs_f.at[1], res_f.at[1], e)
        products(0, True)
        multiply(lhs_a.at[0], res_a.at[0], d)
        products(1, True)
        multiply(lhs_a.at[1], res_a.at[1], e)
        divergence(0, (h1.at[d], h2.at[d]))
        divergence(1, (h1.at[e], h2.at[e]))
        for at in (d, e):
            for copy in results(at):
                copy.start()

    @pl.loop(0, dirs)
    def _(d):
        for copy in results(d):
            copy.wait()

    for copy in last:
        copy.wait()


def params():
    return pltpu.CompilerParams(vmem_limit_bytes=40 * MIB)


def shards(model_one, model_two, weight, direction_one, direction_two):
    dirs = direction_one.shape[0]
    tile = shape(LAYERS, ROWS, LANES)
    ext = shape(LAYERS, EXT, LANES)
    small = shape(LAYERS, 8, LANES)
    fields = (model_one, model_two, weight, direction_one, direction_two)
    mats = pl.pallas_call(
        setup_body,
        out_shape=jax.ShapeDtypeStruct((dirs + 2, 2 * LANES, LANES), jnp.bfloat16),
        cost_estimate=pl.CostEstimate(flops=0, bytes_accessed=8 * MIB, transcendentals=0),
        compiler_params=params(),
        name="setup",
    )()
    any_spec = pl.BlockSpec(memory_space=pl.ANY)
    vmem_spec = pl.BlockSpec(memory_space=pltpu.VMEM)
    xs, xa, e1, e2 = pl.pallas_call(
        functools.partial(pack_body, dirs),
        out_shape=(small, shape(dirs + 3, LAYERS, 8, LANES), tile, tile),
        in_specs=[any_spec] + [vmem_spec] * 5,
        compiler_params=params(),
        name="pack",
    )(mats, *fields)
    count_x, count_y = lax.axis_size("gx"), lax.axis_size("gy")
    xs = lax.ppermute(xs, "gx", swap(count_x, 1))
    xa = lax.ppermute(xa, "gx", swap(count_x, 0))
    xb = pl.pallas_call(
        functools.partial(far_body, dirs),
        out_shape=shape(dirs + 2, LAYERS, 8, LANES),
        in_specs=[any_spec] + [vmem_spec] * 5,
        compiler_params=params(),
        name="far",
    )(xs, *fields)
    xb = lax.ppermute(xb, "gx", swap(count_x, 1))
    e1x, e2x, ya, yb = pl.pallas_call(
        edges_body,
        out_shape=(ext,) * 4,
        compiler_params=params(),
        name="edges",
    )(e1, e2, xa[dirs + 2], xs)
    yb = lax.ppermute(yb, "gy", swap(count_y, 1))
    ya = lax.ppermute(ya, "gy", swap(count_y, 0))
    many = shape(dirs, LAYERS, ROWS, LANES)
    ext_s = scratch(LAYERS, EXT, LANES)
    ext_3 = scratch(3, LAYERS, EXT, LANES)
    tile_s = scratch(LAYERS, ROWS, LANES)
    pair_s = scratch(2, 2, LAYERS, ROWS, LANES)
    many_s = scratch(dirs, LAYERS, ROWS, LANES)
    return pl.pallas_call(
        functools.partial(field_body, dirs),
        out_shape=(tile, tile, many, many),
        out_specs=[pl.BlockSpec(memory_space=pltpu.HBM)] * 4,
        scratch_shapes=[
            tile_s, tile_s, many_s, many_s, pltpu.SemaphoreType.DMA((2, dirs + 1)),
            scratch(2, 2, LAYERS, EXT, LANES), ext_s, ext_3, ext_3, ext_s, ext_s, ext_s, ext_s, tile_s, tile_s,
            scratch(2, 2, LAYERS, EXT, LANES), pair_s, pair_s,
            half(2, 6 * LAYERS * EXT, 2 * LANES), half(2, 6 * LAYERS * ROWS, 2 * LANES),
            scratch(2, 6 * LAYERS * EXT, LANES), scratch(2, 6 * LAYERS * ROWS, LANES),
        ],
        compiler_params=params(),
        name="fields",
    )(mats, *fields, xa, xb, e1x, e2x, ya, yb)


def solution(mesh):
    plane = P(None, "gx", "gy")
    stack = P(None, None, "gx", "gy")
    return jax.shard_map(
        shards,
        mesh=mesh,
        in_specs=(plane, plane, plane, stack, stack),
        out_specs=(plane, plane, stack, stack),
        check_vma=False,
    )
```

```python
import functools

import jax
import jax.numpy as jnp
from jax import lax
from jax.experimental import pallas as pl
from jax.experimental.pallas import tpu as pltpu
from jax.sharding import PartitionSpec as P

LAYERS = 8
ROWS = 16
EXT = 32
LANES = 128
MIB = 1024 * 1024
F32 = jnp.float32


def swap(count, first):
    pairs = []
    for low in range(first, count - 1, 2):
        pairs += [(low, low + 1), (low + 1, low)]
    return pairs


def shape(*dims):
    return jax.ShapeDtypeStruct(dims, F32)


def scratch(*dims):
    return pltpu.VMEM(dims, F32)


def half(*dims):
    return pltpu.VMEM(dims, jnp.bfloat16)


def lane(dims):
    return lax.broadcasted_iota(jnp.int32, dims, len(dims) - 1)


def sub(dims):
    return lax.broadcasted_iota(jnp.int32, dims, len(dims) - 2)


def lroll(value, amount):
    return pltpu.roll(value, amount % LANES, axis=value.ndim - 1)


def sroll(value, amount):
    return pltpu.roll(value, amount % value.shape[-2], axis=value.ndim - 2)


def pack_body(dirs, first, m1, m2, w, d1, d2, e1, e2, ya, yb):
    side = lax.rem(lax.axis_index("gy"), 2)
    block = lane((ROWS, LANES)) // 8
    low = (lane((ROWS, LANES)) % 8) < 4
    for layer in range(LAYERS):
        one = jnp.zeros((ROWS, LANES), F32)
        two = jnp.zeros((ROWS, LANES), F32)
        for d in range(dirs):
            one = jnp.where(block == d, lroll(d1[d, layer], 8 * d + 4), one)
            two = jnp.where(block == d, lroll(d2[d, layer], 8 * d + 4), two)
        one = jnp.where(block == dirs, lroll(m1[layer], 8 * dirs + 4), one)
        one = jnp.where(block == dirs + 1, lroll(w[layer], 8 * dirs + 12), one)
        two = jnp.where(block == dirs + 1, lroll(m2[layer], 8 * dirs + 12), two)
        e1[layer] = one
        e2[layer] = two
        tail = jnp.where(low, one, lroll(two, 4))
        head = jnp.where(low, lroll(two, -4), one)
        ya[layer] = jnp.where(side == 0, tail, head)
        yb[layer] = jnp.where(side == 0, head, tail)


def edge_rows(one, two, tail, layer):
    upper = (sub((8, LANES)) >= 4).astype(jnp.int32)
    start = pl.multiple_of(tail * 8, 8)
    first = one[layer, pl.ds(start, 8), :]
    second = two[layer, pl.ds(start, 8), :]
    return jnp.where(upper == tail, first, sroll(second, 4))


def sides(ya, yb, layer):
    side = lax.rem(lax.axis_index("gy"), 2)
    from_a, from_b = ya[layer], yb[layer]
    left = jnp.where(side == 0, from_b, from_a)
    right = jnp.where(side == 0, from_a, from_b)
    return left, right, lroll(left, -4), lroll(right, 4)


def rows_body(dirs, ya, yb, m1, m2, w, d1, d2, xa, xb, hm):
    core = lax.rem(lax.axis_index("gx"), 2)
    low = (lane((ROWS, LANES)) % 8) < 4
    for layer in range(LAYERS):
        left, right, left2, right2 = sides(ya, yb, layer)
        hm[0, layer] = jnp.where(low, left, right)
        hm[1, layer] = jnp.where(low, left2, right2)
    pairs = [(d1.at[d], d2.at[d]) for d in range(dirs)] + [(m1, m2), (w, w), (hm.at[0], hm.at[1])]
    for index, (one, two) in enumerate(pairs):
        for layer in range(LAYERS):
            xa[index, layer] = edge_rows(one, two, 1 - core, layer)
            xb[index, layer] = edge_rows(one, two, core, layer)


def stencil(up2, up1, down1, down2):
    return 8.0 * (up1 - down1) - (up2 - down2)


def diff_x(ref, layer, start, rows):
    at = lambda offset: ref[layer, pl.ds(start + offset, rows), :]
    return stencil(at(2), at(1), at(-1), at(-2))


def diff_y(value):
    return stencil(lroll(value, -2), lroll(value, -1), lroll(value, 1), lroll(value, 2))


def diff_z(ref, layer, start, rows):
    def at(offset):
        where = layer + offset
        return ref[where, pl.ds(start, rows), :] if 0 <= where < LAYERS else None

    up2, up1, down1, down2 = at(2), at(1), at(-1), at(-2)
    if up1 is None:
        total = -8.0 * down1
    elif down1 is None:
        total = 8.0 * up1
    else:
        total = 8.0 * (up1 - down1)
    if up2 is not None:
        total = total - up2
    if down2 is not None:
        total = total + down2
    return total


def cross(left, right):
    return (
        left[1] * right[2] - left[2] * right[1],
        left[2] * right[0] - left[0] * right[2],
        left[0] * right[1] - left[1] * right[0],
    )


def split3(value):
    high = value.astype(jnp.bfloat16)
    rest = value - high.astype(F32)
    mid = rest.astype(jnp.bfloat16)
    return high, mid, (rest - mid.astype(F32)).astype(jnp.bfloat16)


def band():
    gap = lax.broadcasted_iota(jnp.int32, (LANES, LANES), 0) - lax.broadcasted_iota(jnp.int32, (LANES, LANES), 1)
    near = jnp.where(gap == 1, 8.0, jnp.where(gap == -1, -8.0, 0.0))
    far = jnp.where(gap == 2, -1.0, jnp.where(gap == -2, 1.0, 0.0))
    return (near + far).astype(jnp.bfloat16)


def edge_rows_matrix(block):
    row = lax.broadcasted_iota(jnp.int32, (16, LANES), 0) - 8 * (block % 2)
    col = lax.broadcasted_iota(jnp.int32, (16, LANES), 1)
    table = jnp.zeros((16, LANES), F32)
    for k, c, factor in ((2, 0, 1.0), (3, 0, -8.0), (3, 1, 1.0), (4, 126, -1.0), (4, 127, 8.0), (5, 127, -1.0)):
        table = jnp.where((row == k) & (col == c), factor, table)
    return table.astype(jnp.bfloat16)


def setup_body(mats):
    mats[...] = jnp.zeros(mats.shape, jnp.bfloat16)
    for block in range(mats.shape[0]):
        mats[block, :LANES, :] = band()
        start = LANES + 16 * (block // 2)
        mats[block, start : start + 16, :] = edge_rows_matrix(block)


def phase(dirs, rows, wide, first_row, mats, m1, m2, w, d1, d2, message, hm, hy, outs, done, refs):
    ext_refs, h_ext, w_ext, s1, s2, cor, ax, ay, az, lhs_f, lhs_a, res_f, res_a = refs
    start = first_row + 8
    flat = (LAYERS * rows, LANES)
    flat_out = (LAYERS * wide, LANES)
    main = pl.ds(start, rows)

    def put(lhs, index, value, right=False):
        count = value.shape[0]
        for at, part in enumerate(split3(value)):
            begin = (3 * index + at) * count
            if right:
                lhs[begin : begin + count, LANES:] = part
            else:
                lhs[begin : begin + count, :LANES] = part

    def multiply(lhs, result, block, index=None):
        each = lhs.shape[0] // 2
        span = slice(0, 2 * each) if index is None else slice(index * each, (index + 1) * each)
        result[span] = jnp.dot(lhs[span], mats[block], preferred_element_type=F32)

    def column(result, index, layer):
        per = result.shape[0] // 6
        count = per // LAYERS
        begin = 3 * index * per + layer * count
        part = lambda at: result[begin + at * per : begin + at * per + count]
        return (part(0) + part(1)) + part(2)

    def fill(ext, own, beside, layer):
        ext[layer, 0:8, :] = beside
        ext[layer, 8:24, :] = own[layer]
        ext[layer, 24:32, :] = beside

    def load_ext(slot, one, two, index):
        for layer in range(LAYERS):
            beside = message[index, layer]
            fill(ext_refs.at[slot, 0], one, beside, layer)
            fill(ext_refs.at[slot, 1], two, sroll(beside, 4), layer)
        for k in (0, 1):
            put(lhs_f.at[slot], k, ext_refs[slot, k, :, main, :].reshape(flat))

    for layer in range(LAYERS):
        beside = message[dirs + 2, layer]
        fill(h_ext.at[0], hm.at[0], beside, layer)
        fill(h_ext.at[1], hm.at[1], sroll(beside, 4), layer)
        fill(w_ext, w, message[dirs + 1, layer], layer)
    for k in (0, 1):
        put(lhs_f.at[0], k, h_ext[k, :, main, :].reshape(flat), True)
    load_ext(0, m1, m2, dirs)
    multiply(lhs_f.at[0], res_f.at[0], dirs, 0)
    multiply(lhs_f.at[0], res_f.at[0], dirs + 1, 1)
    for k in (0, 1):
        put(lhs_f.at[1], k, h_ext[k, :, main, :].reshape(flat), True)

    def slopes(slot, k, layer):
        ext = ext_refs.at[slot, k]
        return (
            diff_x(ext, layer, start, rows),
            column(res_f.at[slot], k, layer),
            diff_z(ext, layer, start, rows),
        )

    fold = -1.0 / 20736.0
    block = lane((rows, LANES)) // 8
    within = lane((rows, LANES)) % 8

    def spread(value, at):
        return jnp.take_along_axis(value, within + 8 * at, axis=1)

    for layer in range(LAYERS):
        first, second = (
            (
                diff_x(h_ext.at[k], layer, start, rows),
                hy[k, layer, main, :],
                diff_z(h_ext.at[k], layer, start, rows),
            )
            for k in (0, 1)
        )
        one = tuple(spread(part, dirs) for part in first)
        two = tuple(spread(part, dirs + 1) for part in second)
        weight = spread(h_ext[0, layer, main, :], dirs + 1) * fold
        second = tuple(jnp.where(block == dirs, 0.0, part) for part in second)
        left_term = cross(first, two)
        right_term = cross(one, second)
        rw = tuple(weight * (left_term[i] + right_term[i]) for i in range(3))
        cor[0, layer, :rows, :] = cross(two, rw)[1]
        cor[1, layer, :rows, :] = cross(rw, one)[1]
    for slot in (0, 1):
        for k in (0, 1):
            put(lhs_a.at[slot], k, cor[k, :, 2 : 2 + wide, :].reshape(flat_out), True)

    for layer in range(LAYERS):
        for k, ref in ((0, s1), (1, s2)):
            for index, part in enumerate(slopes(0, k, layer)):
                ref[index, layer] = part

    def products(slot, second_field):
        for layer in range(LAYERS):
            one = (s1[0, layer], s1[1, layer], s1[2, layer])
            two = (s2[0, layer], s2[1, layer], s2[2, layer])
            if second_field:
                perturbed = tuple(
                    p + q for p, q in zip(cross(slopes(slot, 0, layer), two), cross(one, slopes(slot, 1, layer)))
                )
            else:
                perturbed = cross(one, two)
            weight = w_ext[layer, main, :] * fold
            rw = tuple(weight * part for part in perturbed)
            for k, adj in ((0, cross(two, rw)), (1, cross(rw, one))):
                ax[slot, k, layer, :rows, :] = adj[0]
                ay[slot, k, layer, :rows, :] = adj[1]
                az[slot, k, layer, :rows, :] = adj[2]
        for k in (0, 1):
            put(lhs_a.at[slot], k, ay[slot, k, :, 2 : 2 + wide, :].reshape(flat_out))

    def divergence(slot, targets):
        for k in (0, 1):
            for layer in range(LAYERS):
                total = (
                    diff_x(ax.at[slot, k], layer, 2, wide)
                    + column(res_a.at[slot], k, layer)
                    + diff_z(az.at[slot, k], layer, 2, wide)
                )
                targets[k][layer, pl.ds(first_row + 2, rows - 4), :] = total[: rows - 4]

    g1, g2, h1, h2 = outs
    products(0, False)
    multiply(lhs_a.at[0], res_a.at[0], dirs)
    divergence(0, (g1, g2))
    done(None)

    @pl.loop(0, dirs // 2)
    def _(step):
        d, e = 2 * step, 2 * step + 1
        load_ext(0, d1.at[d], d2.at[d], d)
        multiply(lhs_f.at[0], res_f.at[0], d)
        load_ext(1, d1.at[e], d2.at[e], e)
        multiply(lhs_f.at[1], res_f.at[1], e)
        products(0, True)
        multiply(lhs_a.at[0], res_a.at[0], d)
        products(1, True)
        multiply(lhs_a.at[1], res_a.at[1], e)
        divergence(0, (h1.at[d], h2.at[d]))
        divergence(1, (h1.at[e], h2.at[e]))
        done(d)
        done(e)


def phase_scratch(rows, wide):
    ext = scratch(LAYERS, EXT, LANES)
    slopes = scratch(3, LAYERS, rows, LANES)
    adjoint = scratch(2, 2, LAYERS, rows + 16, LANES)
    return [
        scratch(2, 2, LAYERS, EXT, LANES), scratch(2, LAYERS, EXT, LANES), ext, slopes, slopes,
        scratch(2, LAYERS, rows + 16, LANES), adjoint, adjoint, adjoint,
        half(2, 6 * LAYERS * rows, 2 * LANES), half(2, 6 * LAYERS * wide, 2 * LANES),
        scratch(2, 6 * LAYERS * rows, LANES), scratch(2, 6 * LAYERS * wide, LANES),
    ]


def near_body(dirs, mats, m1, m2, w, d1, d2, xa, hm, e1, e2, ya, yb, g1, g2, h1, h2, hy, *refs):
    core = lax.rem(lax.axis_index("gx"), 2)
    low = (lane((ROWS, LANES)) % 8) < 4
    for layer in range(LAYERS):
        left, right, left2, right2 = sides(ya, yb, layer)
        for k, own, before, after in ((0, e1[layer], left, right), (1, e2[layer], left2, right2)):
            before = diff_y(jnp.where(low, before, own))
            after = diff_y(jnp.where(low, own, after))
            hy[k, layer, 8:24, :] = jnp.where(low, before, after)
            hy[k, layer, 0:8, :] = jnp.zeros((8, LANES), F32)
            hy[k, layer, 24:32, :] = jnp.zeros((8, LANES), F32)
    phase(
        dirs, 16, 16, 2 - 4 * core, mats, m1, m2, w, d1, d2, xa, hm, hy, (g1, g2, h1, h2), lambda d: None, refs
    )


def rest_body(
    dirs, mats, m1, m2, w, d1, d2, xb, hm, hy, g1_in, g2_in, h1_in, h2_in,
    g1_out, g2_out, h1_out, h2_out, g1, g2, h1, h2, sems, *refs,
):
    core = lax.rem(lax.axis_index("gx"), 2)

    def copies(d):
        if d is None:
            return (
                pltpu.make_async_copy(g1, g1_out, sems.at[0, dirs]),
                pltpu.make_async_copy(g2, g2_out, sems.at[1, dirs]),
            )
        return (
            pltpu.make_async_copy(h1.at[d], h1_out.at[d], sems.at[0, d]),
            pltpu.make_async_copy(h2.at[d], h2_out.at[d], sems.at[1, d]),
        )

    def done(d):
        for copy in copies(d):
            copy.start()

    g1[...] = g1_in[...]
    g2[...] = g2_in[...]
    h1[...] = h1_in[...]
    h2[...] = h2_in[...]
    phase(dirs, 8, 8, 12 * core - 2, mats, m1, m2, w, d1, d2, xb, hm, hy, (g1, g2, h1, h2), done, refs)

    @pl.loop(0, dirs)
    def _(d):
        for copy in copies(d):
            copy.wait()

    for copy in copies(None):
        copy.wait()


def params():
    return pltpu.CompilerParams(vmem_limit_bytes=40 * MIB)


def cost(mib):
    return pl.CostEstimate(flops=0, bytes_accessed=mib * MIB, transcendentals=0)


def shards(model_one, model_two, weight, direction_one, direction_two):
    dirs = direction_one.shape[0]
    tile = shape(LAYERS, ROWS, LANES)
    many = shape(dirs, LAYERS, ROWS, LANES)
    message = shape(dirs + 3, LAYERS, 8, LANES)
    tile_s = scratch(LAYERS, ROWS, LANES)
    many_s = scratch(dirs, LAYERS, ROWS, LANES)
    fields = (model_one, model_two, weight, direction_one, direction_two)
    count_x, count_y = lax.axis_size("gx"), lax.axis_size("gy")
    any_spec = pl.BlockSpec(memory_space=pl.ANY)
    vmem_spec = pl.BlockSpec(memory_space=pltpu.VMEM)
    mats = pl.pallas_call(
        setup_body,
        out_shape=jax.ShapeDtypeStruct((dirs + 2, 2 * LANES, LANES), jnp.bfloat16),
        cost_estimate=cost(64),
        compiler_params=params(),
        name="setup",
    )()
    e1, e2, ya, yb = pl.pallas_call(
        functools.partial(pack_body, dirs),
        out_shape=(tile,) * 4,
        in_specs=[any_spec] + [vmem_spec] * 5,
        compiler_params=params(),
        name="pack",
    )(mats, *fields)
    yb = lax.ppermute(yb, "gy", swap(count_y, 1))
    ya = lax.ppermute(ya, "gy", swap(count_y, 0))
    xa, xb, hm = pl.pallas_call(
        functools.partial(rows_body, dirs),
        out_shape=(message, message, shape(2, LAYERS, ROWS, LANES)),
        compiler_params=params(),
        name="rows",
    )(ya, yb, *fields)
    xb = lax.ppermute(xb, "gx", swap(count_x, 1))
    xa = lax.ppermute(xa, "gx", swap(count_x, 0))
    g1, g2, h1, h2, hy = pl.pallas_call(
        functools.partial(near_body, dirs),
        out_shape=(tile, tile, many, many, shape(2, LAYERS, EXT, LANES)),
        scratch_shapes=phase_scratch(16, 16),
        cost_estimate=cost(16),
        compiler_params=params(),
        name="near",
    )(mats, *fields, xa, hm, e1, e2, ya, yb)
    return pl.pallas_call(
        functools.partial(rest_body, dirs),
        out_shape=(tile, tile, many, many),
        out_specs=[pl.BlockSpec(memory_space=pltpu.HBM)] * 4,
        scratch_shapes=[tile_s, tile_s, many_s, many_s, pltpu.SemaphoreType.DMA((2, dirs + 1))] + phase_scratch(8, 8),
        cost_estimate=cost(8),
        compiler_params=params(),
        name="rest",
    )(mats, *fields, xb, hm, hy, g1, g2, h1, h2)


def solution(mesh):
    plane = P(None, "gx", "gy")
    stack = P(None, None, "gx", "gy")
    return jax.shard_map(
        shards,
        mesh=mesh,
        in_specs=(plane, plane, plane, stack, stack),
        out_specs=(plane, plane, stack, stack),
        check_vma=False,
    )
```

```python
import functools

import jax
import jax.numpy as jnp
from jax import lax
from jax.experimental import pallas as pl
from jax.experimental.pallas import tpu as pltpu
from jax.sharding import PartitionSpec as P

LAYERS = 8
ROWS = 16
EXT = 32
LANES = 128
MIB = 1024 * 1024
NEAR_SLOTS = 2
REST_SLOTS = 5
F32 = jnp.float32


def swap(count, first):
    pairs = []
    for low in range(first, count - 1, 2):
        pairs += [(low, low + 1), (low + 1, low)]
    return pairs


def shape(*dims):
    return jax.ShapeDtypeStruct(dims, F32)


def scratch(*dims):
    return pltpu.VMEM(dims, F32)


def half(*dims):
    return pltpu.VMEM(dims, jnp.bfloat16)


def lane(dims):
    return lax.broadcasted_iota(jnp.int32, dims, len(dims) - 1)


def sub(dims):
    return lax.broadcasted_iota(jnp.int32, dims, len(dims) - 2)


def lroll(value, amount):
    return pltpu.roll(value, amount % LANES, axis=value.ndim - 1)


def sroll(value, amount):
    return pltpu.roll(value, amount % value.shape[-2], axis=value.ndim - 2)


def split(dirs, fields):
    return (
        fields.at[dirs],
        fields.at[2 * dirs + 1],
        fields.at[2 * dirs + 2],
        fields.at[pl.ds(0, dirs)],
        fields.at[pl.ds(dirs + 1, dirs)],
    )


def pack_body(dirs, fields, e1, e2, ya, yb):
    m1, m2, w, d1, d2 = split(dirs, fields)
    side = lax.rem(lax.axis_index("gy"), 2)
    block = lane((ROWS, LANES)) // 8
    low = (lane((ROWS, LANES)) % 8) < 4
    for layer in range(LAYERS):
        one = jnp.zeros((ROWS, LANES), F32)
        two = jnp.zeros((ROWS, LANES), F32)
        for d in range(dirs):
            one = jnp.where(block == d, lroll(d1[d, layer], 8 * d + 4), one)
            two = jnp.where(block == d, lroll(d2[d, layer], 8 * d + 4), two)
        one = jnp.where(block == dirs, lroll(m1[layer], 8 * dirs + 4), one)
        one = jnp.where(block == dirs + 1, lroll(w[layer], 8 * dirs + 12), one)
        two = jnp.where(block == dirs + 1, lroll(m2[layer], 8 * dirs + 12), two)
        e1[layer] = one
        e2[layer] = two
        tail = jnp.where(low, one, lroll(two, 4))
        head = jnp.where(low, lroll(two, -4), one)
        ya[layer] = jnp.where(side == 0, tail, head)
        yb[layer] = jnp.where(side == 0, head, tail)


def edge_rows(one, two, tail, layer):
    upper = (sub((8, LANES)) >= 4).astype(jnp.int32)
    start = pl.multiple_of(tail * 8, 8)
    first = one[layer, pl.ds(start, 8), :]
    second = two[layer, pl.ds(start, 8), :]
    return jnp.where(upper == tail, first, sroll(second, 4))


def sides(ya, yb, layer):
    side = lax.rem(lax.axis_index("gy"), 2)
    from_a, from_b = ya[layer], yb[layer]
    left = jnp.where(side == 0, from_b, from_a)
    right = jnp.where(side == 0, from_a, from_b)
    return left, right, lroll(left, -4), lroll(right, 4)


def rows_body(dirs, ya, yb, fields, xb, hm):
    low = (lane((ROWS, LANES)) % 8) < 4
    for layer in range(LAYERS):
        left, right, left2, right2 = sides(ya, yb, layer)
        hm[0, layer] = jnp.where(low, left, right)
        hm[1, layer] = jnp.where(low, left2, right2)
    message_rows(dirs, lax.rem(lax.axis_index("gx"), 2), fields, hm, (xb, xb.at[pl.ds(dirs, 3)]))


def message_rows(dirs, tail, fields, hm, out):
    m1, m2, w, d1, d2 = split(dirs, fields)
    pairs = [(d1.at[d], d2.at[d]) for d in range(dirs)] + [(m1, m2), (w, w), (hm.at[0], hm.at[1])]
    for index, (one, two) in enumerate(pairs):
        for layer in range(LAYERS):
            target = out[0].at[index] if index < dirs else out[1].at[index - dirs]
            target[layer] = edge_rows(one, two, tail, layer)


def core_body(dirs, fields, hm, xa, xa_rest):
    message_rows(dirs, 1 - lax.rem(lax.axis_index("gx"), 2), fields, hm, (xa, xa_rest))


def stencil(up2, up1, down1, down2):
    return 8.0 * (up1 - down1) - (up2 - down2)


def diff_x(ref, layer, start, rows):
    at = lambda offset: ref[layer, pl.ds(start + offset, rows), :]
    return stencil(at(2), at(1), at(-1), at(-2))


def diff_y(value):
    return stencil(lroll(value, -2), lroll(value, -1), lroll(value, 1), lroll(value, 2))


def layers_of(ref, start, rows):
    held = {}

    def at(layer):
        if not 0 <= layer < LAYERS:
            return None
        if layer not in held:
            held[layer] = ref[layer, pl.ds(start, rows), :]
        return held[layer]

    return at


def diff_z(at, layer):
    up2, up1, down1, down2 = at(layer + 2), at(layer + 1), at(layer - 1), at(layer - 2)
    if up1 is None:
        total = -8.0 * down1
    elif down1 is None:
        total = 8.0 * up1
    else:
        total = 8.0 * (up1 - down1)
    if up2 is not None:
        total = total - up2
    if down2 is not None:
        total = total + down2
    return total


def cross(left, right):
    return (
        left[1] * right[2] - left[2] * right[1],
        left[2] * right[0] - left[0] * right[2],
        left[0] * right[1] - left[1] * right[0],
    )


def split3(value):
    high = value.astype(jnp.bfloat16)
    rest = value - high.astype(F32)
    mid = rest.astype(jnp.bfloat16)
    return high, mid, (rest - mid.astype(F32)).astype(jnp.bfloat16)


def band():
    gap = lax.broadcasted_iota(jnp.int32, (LANES, LANES), 0) - lax.broadcasted_iota(jnp.int32, (LANES, LANES), 1)
    near = jnp.where(gap == 1, 8.0, jnp.where(gap == -1, -8.0, 0.0))
    far = jnp.where(gap == 2, -1.0, jnp.where(gap == -2, 1.0, 0.0))
    return (near + far).astype(jnp.bfloat16)


def edge_rows_matrix(block):
    row = lax.broadcasted_iota(jnp.int32, (16, LANES), 0) - 8 * (block % 2)
    col = lax.broadcasted_iota(jnp.int32, (16, LANES), 1)
    table = jnp.zeros((16, LANES), F32)
    for k, c, factor in ((2, 0, 1.0), (3, 0, -8.0), (3, 1, 1.0), (4, 126, -1.0), (4, 127, 8.0), (5, 127, -1.0)):
        table = jnp.where((row == k) & (col == c), factor, table)
    return table.astype(jnp.bfloat16)


def setup_body(mats):
    mats[...] = jnp.zeros(mats.shape, jnp.bfloat16)
    for block in range(mats.shape[0]):
        mats[block, :LANES, :] = band()
        start = LANES + 16 * (block // 2)
        mats[block, start : start + 16, :] = edge_rows_matrix(block)


def phase(dirs, rows, wide, slots, first_row, after, mats, fields, message, hm, hy, outs, done, refs):
    m1, m2, w, d1, d2 = split(dirs, fields)
    ext_refs, h_ext, w_ext, s1, s2, cor, ax, ay, az, lhs_f, lhs_a, res_f, res_a = refs
    start = first_row + 8
    flat = (LAYERS * rows, LANES)
    flat_out = (LAYERS * wide, LANES)
    main = pl.ds(start, rows)

    def put(lhs, index, value, right=False):
        count = value.shape[0]
        for at, part in enumerate(split3(value)):
            begin = (3 * index + at) * count
            if right:
                lhs[begin : begin + count, LANES:] = part
            else:
                lhs[begin : begin + count, :LANES] = part

    def multiply(lhs, result, block, index=None):
        each = lhs.shape[0] // 2
        span = slice(0, 2 * each) if index is None else slice(index * each, (index + 1) * each)
        result[span] = jnp.dot(lhs[span], mats[block], preferred_element_type=F32)

    def column(result, index, layer):
        per = result.shape[0] // 6
        count = per // LAYERS
        begin = 3 * index * per + layer * count
        part = lambda at: result[begin + at * per : begin + at * per + count]
        return (part(0) + part(1)) + part(2)

    def fill(ext, own, beside, layer):
        ext[layer, pl.ds(pl.multiple_of(24 * after, 8), 8), :] = beside
        if rows == ROWS:
            ext[layer, 8:24, :] = own[layer]
        else:
            begin = pl.multiple_of(8 * after, 8)
            ext[layer, pl.ds(begin + 8, 8), :] = own[layer, pl.ds(begin, 8), :]

    def load_ext(slot, one, two, source):
        for layer in range(LAYERS):
            beside = source[layer]
            fill(ext_refs.at[slot, 0], one, beside, layer)
            fill(ext_refs.at[slot, 1], two, sroll(beside, 4), layer)
        for k in (0, 1):
            put(lhs_f.at[slot], k, ext_refs[slot, k, :, main, :].reshape(flat))

    for layer in range(LAYERS):
        beside = message[1][2, layer]
        fill(h_ext.at[0], hm.at[0], beside, layer)
        fill(h_ext.at[1], hm.at[1], sroll(beside, 4), layer)
        fill(w_ext, w, message[1][1, layer], layer)
    for k in (0, 1):
        put(lhs_f.at[0], k, h_ext[k, :, main, :].reshape(flat), True)
    load_ext(0, m1, m2, message[1].at[0])
    multiply(lhs_f.at[0], res_f.at[0], dirs, 0)
    multiply(lhs_f.at[0], res_f.at[0], dirs + 1, 1)
    for slot in range(1, slots):
        for k in (0, 1):
            put(lhs_f.at[slot], k, h_ext[k, :, main, :].reshape(flat), True)

    def slopes(slot, k, layer, layers):
        return (
            diff_x(ext_refs.at[slot, k], layer, start, rows),
            column(res_f.at[slot], k, layer),
            diff_z(layers, layer),
        )

    def loaded(slot):
        return tuple(layers_of(ext_refs.at[slot, k], start, rows) for k in (0, 1))

    fold = -1.0 / 20736.0
    block = lane((rows, LANES)) // 8
    within = lane((rows, LANES)) % 8

    def spread(value, at):
        return jnp.take_along_axis(value, within + 8 * at, axis=1)

    packed = tuple(layers_of(h_ext.at[k], start, rows) for k in (0, 1))
    for layer in range(LAYERS):
        first, second = (
            (
                diff_x(h_ext.at[k], layer, start, rows),
                hy[k, layer, main, :],
                diff_z(packed[k], layer),
            )
            for k in (0, 1)
        )
        one = tuple(spread(part, dirs) for part in first)
        two = tuple(spread(part, dirs + 1) for part in second)
        weight = spread(h_ext[0, layer, main, :], dirs + 1) * fold
        second = tuple(jnp.where(block == dirs, 0.0, part) for part in second)
        left_term = cross(first, two)
        right_term = cross(one, second)
        rw = tuple(weight * (left_term[i] + right_term[i]) for i in range(3))
        cor[0, layer, :rows, :] = cross(two, rw)[1]
        cor[1, layer, :rows, :] = cross(rw, one)[1]
    for slot in range(slots):
        for k in (0, 1):
            put(lhs_a.at[slot], k, cor[k, :, 2 : 2 + wide, :].reshape(flat_out), True)

    models = loaded(0)
    for layer in range(LAYERS):
        for k, ref in ((0, s1), (1, s2)):
            for index, part in enumerate(slopes(0, k, layer, models[k])):
                ref[index, layer] = part

    def products(slot, second_field):
        held = loaded(slot)
        for layer in range(LAYERS):
            one = (s1[0, layer], s1[1, layer], s1[2, layer])
            two = (s2[0, layer], s2[1, layer], s2[2, layer])
            if second_field:
                perturbed = tuple(
                    p + q
                    for p, q in zip(
                        cross(slopes(slot, 0, layer, held[0]), two), cross(one, slopes(slot, 1, layer, held[1]))
                    )
                )
            else:
                perturbed = cross(one, two)
            weight = w_ext[layer, main, :] * fold
            rw = tuple(weight * part for part in perturbed)
            for k, adj in ((0, cross(two, rw)), (1, cross(rw, one))):
                ax[slot, k, layer, :rows, :] = adj[0]
                ay[slot, k, layer, :rows, :] = adj[1]
                az[slot, k, layer, :rows, :] = adj[2]
        for k in (0, 1):
            put(lhs_a.at[slot], k, ay[slot, k, :, 2 : 2 + wide, :].reshape(flat_out))

    def divergence(slot, targets):
        for k in (0, 1):
            layers = layers_of(az.at[slot, k], 2, wide)
            for layer in range(LAYERS):
                total = (
                    diff_x(ax.at[slot, k], layer, 2, wide)
                    + column(res_a.at[slot], k, layer)
                    + diff_z(layers, layer)
                )
                targets[k][layer, pl.ds(first_row + 2, rows - 4), :] = total[: rows - 4]

    g1, g2, h1, h2 = outs
    products(0, False)
    multiply(lhs_a.at[0], res_a.at[0], dirs)
    divergence(0, (g1, g2))
    done(None)

    def batch(begin, count):
        for slot in range(count):
            load_ext(slot, d1.at[begin + slot], d2.at[begin + slot], message[0].at[begin + slot])
            multiply(lhs_f.at[slot], res_f.at[slot], begin + slot)
        for slot in range(count):
            products(slot, True)
            multiply(lhs_a.at[slot], res_a.at[slot], begin + slot)
        for slot in range(count):
            divergence(slot, (h1.at[begin + slot], h2.at[begin + slot]))
            done(begin + slot)

    @pl.loop(0, dirs // slots)
    def _(step):
        batch(step * slots, slots)

    if dirs % slots:
        batch(dirs - dirs % slots, dirs % slots)


def phase_scratch(rows, wide, slots):
    ext = scratch(LAYERS, EXT, LANES)
    slopes = scratch(3, LAYERS, rows, LANES)
    adjoint = scratch(slots, 2, LAYERS, rows + 16, LANES)
    return [
        scratch(slots, 2, LAYERS, EXT, LANES), scratch(2, LAYERS, EXT, LANES), ext, slopes, slopes,
        scratch(2, LAYERS, rows + 16, LANES), adjoint, adjoint, adjoint,
        half(slots, 6 * LAYERS * rows, 2 * LANES), half(slots, 6 * LAYERS * wide, 2 * LANES),
        scratch(slots, 6 * LAYERS * rows, LANES), scratch(slots, 6 * LAYERS * wide, LANES),
    ]


def near_body(dirs, mats, fields, xa, xa_rest, hm, e1, e2, ya, yb, g1, g2, h1, h2, hy, *refs):
    core = lax.rem(lax.axis_index("gx"), 2)
    low = (lane((ROWS, LANES)) % 8) < 4
    for layer in range(LAYERS):
        left, right, left2, right2 = sides(ya, yb, layer)
        for k, own, before, after in ((0, e1[layer], left, right), (1, e2[layer], left2, right2)):
            before = diff_y(jnp.where(low, before, own))
            after = diff_y(jnp.where(low, own, after))
            hy[k, layer, 8:24, :] = jnp.where(low, before, after)
            hy[k, layer, 0:8, :] = jnp.zeros((8, LANES), F32)
            hy[k, layer, 24:32, :] = jnp.zeros((8, LANES), F32)
    phase(
        dirs, 16, 16, NEAR_SLOTS, 2 - 4 * core, 1 - core, mats, fields, (xa, xa_rest), hm, hy, (g1, g2, h1, h2), lambda d: None, refs
    )


def rest_body(
    dirs, mats, fields, xb, hm, hy, g1_in, g2_in, h1_in, h2_in,
    g1_out, g2_out, h1_out, h2_out, g1, g2, h1, h2, sems, *refs,
):
    core = lax.rem(lax.axis_index("gx"), 2)

    def copies(d):
        if d is None:
            return (
                pltpu.make_async_copy(g1, g1_out, sems.at[0, dirs]),
                pltpu.make_async_copy(g2, g2_out, sems.at[1, dirs]),
            )
        return (
            pltpu.make_async_copy(h1.at[d], h1_out.at[d], sems.at[0, d]),
            pltpu.make_async_copy(h2.at[d], h2_out.at[d], sems.at[1, d]),
        )

    def done(d):
        for copy in copies(d):
            copy.start()

    g1[...] = g1_in[...]
    g2[...] = g2_in[...]
    h1[...] = h1_in[...]
    h2[...] = h2_in[...]
    phase(dirs, 8, 8, REST_SLOTS, 12 * core - 2, core, mats, fields, (xb, xb.at[pl.ds(dirs, 3)]), hm, hy, (g1, g2, h1, h2), done, refs)

    @pl.loop(0, dirs)
    def _(d):
        for copy in copies(d):
            copy.wait()

    for copy in copies(None):
        copy.wait()


def params():
    return pltpu.CompilerParams(vmem_limit_bytes=40 * MIB)


def cost(mib):
    return pl.CostEstimate(flops=0, bytes_accessed=mib * MIB, transcendentals=0)


def shards(model_one, model_two, weight, direction_one, direction_two):
    dirs = direction_one.shape[0]
    tile = shape(LAYERS, ROWS, LANES)
    many = shape(dirs, LAYERS, ROWS, LANES)
    message = shape(dirs + 3, LAYERS, 8, LANES)
    many_rows, few_rows = shape(dirs, LAYERS, 8, LANES), shape(3, LAYERS, 8, LANES)
    tile_s = scratch(LAYERS, ROWS, LANES)
    many_s = scratch(dirs, LAYERS, ROWS, LANES)
    fields = jnp.concatenate(
        [direction_one, model_one[None], direction_two, model_two[None], weight[None]], 0
    )
    count_x, count_y = lax.axis_size("gx"), lax.axis_size("gy")
    mats = pl.pallas_call(
        setup_body,
        out_shape=jax.ShapeDtypeStruct((dirs + 2, 2 * LANES, LANES), jnp.bfloat16),
        cost_estimate=cost(64),
        compiler_params=params(),
        name="setup",
    )()
    e1, e2, ya, yb = pl.pallas_call(
        functools.partial(pack_body, dirs),
        out_shape=(tile,) * 4,
        compiler_params=params(),
        name="pack",
    )(fields)
    yb = lax.ppermute(yb, "gy", swap(count_y, 1))
    ya = lax.ppermute(ya, "gy", swap(count_y, 0))
    xb, hm = pl.pallas_call(
        functools.partial(rows_body, dirs),
        out_shape=(message, shape(2, LAYERS, ROWS, LANES)),
        compiler_params=params(),
        name="rows",
    )(ya, yb, fields)
    xb = lax.ppermute(xb, "gx", swap(count_x, 1))
    xa, xa_rest = pl.pallas_call(
        functools.partial(core_body, dirs),
        out_shape=(many_rows, few_rows),
        cost_estimate=cost(4),
        compiler_params=params(),
        name="core",
    )(fields, hm)
    xa = lax.ppermute(xa, "gx", swap(count_x, 0))
    xa_rest = lax.ppermute(xa_rest, "gx", swap(count_x, 0))
    g1, g2, h1, h2, hy = pl.pallas_call(
        functools.partial(near_body, dirs),
        out_shape=(tile, tile, many, many, shape(2, LAYERS, EXT, LANES)),
        scratch_shapes=phase_scratch(16, 16, NEAR_SLOTS),
        cost_estimate=cost(16),
        compiler_params=params(),
        name="near",
    )(mats, fields, xa, xa_rest, hm, e1, e2, ya, yb)
    return pl.pallas_call(
        functools.partial(rest_body, dirs),
        out_shape=(tile, tile, many, many),
        out_specs=[pl.BlockSpec(memory_space=pltpu.HBM)] * 4,
        scratch_shapes=[tile_s, tile_s, many_s, many_s, pltpu.SemaphoreType.DMA((2, dirs + 1))] + phase_scratch(8, 8, REST_SLOTS),
        cost_estimate=cost(8),
        compiler_params=params(),
        name="rest",
    )(mats, fields, xb, hm, hy, g1, g2, h1, h2)


def solution(mesh):
    plane = P(None, "gx", "gy")
    stack = P(None, None, "gx", "gy")
    return jax.shard_map(
        shards,
        mesh=mesh,
        in_specs=(plane, plane, plane, stack, stack),
        out_specs=(plane, plane, stack, stack),
        check_vma=False,
    )
```

```python
import functools

import jax
import jax.numpy as jnp
from jax import lax
from jax.experimental import pallas as pl
from jax.experimental.pallas import tpu as pltpu
from jax.sharding import PartitionSpec as P

LAYERS = 8
ROWS = 16
EXT = 32
LANES = 128
MIB = 1024 * 1024
NEAR_SLOTS = 5
REST_SLOTS = 10
F32 = jnp.float32


def swap(count, first):
    pairs = []
    for low in range(first, count - 1, 2):
        pairs += [(low, low + 1), (low + 1, low)]
    return pairs


def shape(*dims):
    return jax.ShapeDtypeStruct(dims, F32)


def scratch(*dims):
    return pltpu.VMEM(dims, F32)


def half(*dims):
    return pltpu.VMEM(dims, jnp.bfloat16)


def lane(dims):
    return lax.broadcasted_iota(jnp.int32, dims, len(dims) - 1)


def sub(dims):
    return lax.broadcasted_iota(jnp.int32, dims, len(dims) - 2)


def lroll(value, amount):
    return pltpu.roll(value, amount % LANES, axis=value.ndim - 1)


def sroll(value, amount):
    return pltpu.roll(value, amount % value.shape[-2], axis=value.ndim - 2)


def split(dirs, fields):
    return (
        fields.at[dirs],
        fields.at[2 * dirs + 1],
        fields.at[2 * dirs + 2],
        fields.at[pl.ds(0, dirs)],
        fields.at[pl.ds(dirs + 1, dirs)],
    )


def pack_body(dirs, fields, e1, e2, ya, yb):
    m1, m2, w, d1, d2 = split(dirs, fields)
    side = lax.rem(lax.axis_index("gy"), 2)
    block = lane((ROWS, LANES)) // 8
    low = (lane((ROWS, LANES)) % 8) < 4
    for layer in range(LAYERS):
        one = jnp.zeros((ROWS, LANES), F32)
        two = jnp.zeros((ROWS, LANES), F32)
        for d in range(dirs):
            one = jnp.where(block == d, lroll(d1[d, layer], 8 * d + 4), one)
            two = jnp.where(block == d, lroll(d2[d, layer], 8 * d + 4), two)
        one = jnp.where(block == dirs, lroll(m1[layer], 8 * dirs + 4), one)
        one = jnp.where(block == dirs + 1, lroll(w[layer], 8 * dirs + 12), one)
        two = jnp.where(block == dirs + 1, lroll(m2[layer], 8 * dirs + 12), two)
        e1[layer] = one
        e2[layer] = two
        tail = jnp.where(low, one, lroll(two, 4))
        head = jnp.where(low, lroll(two, -4), one)
        ya[layer] = jnp.where(side == 0, tail, head)
        yb[layer] = jnp.where(side == 0, head, tail)


def edge_rows(one, two, tail, layer):
    upper = (sub((8, LANES)) >= 4).astype(jnp.int32)
    start = pl.multiple_of(tail * 8, 8)
    first = one[layer, pl.ds(start, 8), :]
    second = two[layer, pl.ds(start, 8), :]
    return jnp.where(upper == tail, first, sroll(second, 4))


def sides(ya, yb, layer):
    side = lax.rem(lax.axis_index("gy"), 2)
    from_a, from_b = ya[layer], yb[layer]
    left = jnp.where(side == 0, from_b, from_a)
    right = jnp.where(side == 0, from_a, from_b)
    return left, right, lroll(left, -4), lroll(right, 4)


def rows_body(dirs, ya, yb, fields, xb, hm):
    low = (lane((ROWS, LANES)) % 8) < 4
    for layer in range(LAYERS):
        left, right, left2, right2 = sides(ya, yb, layer)
        hm[0, layer] = jnp.where(low, left, right)
        hm[1, layer] = jnp.where(low, left2, right2)
    message_rows(dirs, lax.rem(lax.axis_index("gx"), 2), fields, hm, (xb, xb.at[pl.ds(dirs, 3)]))


def message_rows(dirs, tail, fields, hm, out):
    m1, m2, w, d1, d2 = split(dirs, fields)
    pairs = [(d1.at[d], d2.at[d]) for d in range(dirs)] + [(m1, m2), (w, w), (hm.at[0], hm.at[1])]
    for index, (one, two) in enumerate(pairs):
        for layer in range(LAYERS):
            target = out[0].at[index] if index < dirs else out[1].at[index - dirs]
            target[layer] = edge_rows(one, two, tail, layer)


def core_body(dirs, fields, hm, xa, xa_rest):
    message_rows(dirs, 1 - lax.rem(lax.axis_index("gx"), 2), fields, hm, (xa, xa_rest))


def stencil(up2, up1, down1, down2):
    return 8.0 * (up1 - down1) - (up2 - down2)


def diff_x(ref, layer, start, rows):
    at = lambda offset: ref[layer, pl.ds(start + offset, rows), :]
    return stencil(at(2), at(1), at(-1), at(-2))


def diff_y(value):
    return stencil(lroll(value, -2), lroll(value, -1), lroll(value, 1), lroll(value, 2))


def layers_of(ref, start, rows):
    held = {}

    def at(layer):
        if not 0 <= layer < LAYERS:
            return None
        if layer not in held:
            held[layer] = ref[layer, pl.ds(start, rows), :]
        return held[layer]

    return at


def diff_z(at, layer):
    up2, up1, down1, down2 = at(layer + 2), at(layer + 1), at(layer - 1), at(layer - 2)
    if up1 is None:
        total = -8.0 * down1
    elif down1 is None:
        total = 8.0 * up1
    else:
        total = 8.0 * (up1 - down1)
    if up2 is not None:
        total = total - up2
    if down2 is not None:
        total = total + down2
    return total


def cross(left, right):
    return (
        left[1] * right[2] - left[2] * right[1],
        left[2] * right[0] - left[0] * right[2],
        left[0] * right[1] - left[1] * right[0],
    )


def split3(value):
    high = value.astype(jnp.bfloat16)
    rest = value - high.astype(F32)
    mid = rest.astype(jnp.bfloat16)
    return high, mid, (rest - mid.astype(F32)).astype(jnp.bfloat16)


def band():
    gap = lax.broadcasted_iota(jnp.int32, (LANES, LANES), 0) - lax.broadcasted_iota(jnp.int32, (LANES, LANES), 1)
    near = jnp.where(gap == 1, 8.0, jnp.where(gap == -1, -8.0, 0.0))
    far = jnp.where(gap == 2, -1.0, jnp.where(gap == -2, 1.0, 0.0))
    return (near + far).astype(jnp.bfloat16)


def edge_rows_matrix(block):
    row = lax.broadcasted_iota(jnp.int32, (16, LANES), 0) - 8 * (block % 2)
    col = lax.broadcasted_iota(jnp.int32, (16, LANES), 1)
    table = jnp.zeros((16, LANES), F32)
    for k, c, factor in ((2, 0, 1.0), (3, 0, -8.0), (3, 1, 1.0), (4, 126, -1.0), (4, 127, 8.0), (5, 127, -1.0)):
        table = jnp.where((row == k) & (col == c), factor, table)
    return table.astype(jnp.bfloat16)


def setup_body(mats):
    mats[...] = jnp.zeros(mats.shape, jnp.bfloat16)
    for block in range(mats.shape[0]):
        mats[block, :LANES, :] = band()
        start = LANES + 16 * (block // 2)
        mats[block, start : start + 16, :] = edge_rows_matrix(block)


def phase(dirs, rows, wide, slots, first_row, after, mats, fields, message, hm, hy, outs, done, refs):
    m1, m2, w, d1, d2 = split(dirs, fields)
    ext_refs, h_ext, w_ext, s1, s2, cor, ax, ay, az, lhs_f, lhs_a, res_f, res_a = refs
    start = first_row + 8
    main = pl.ds(start, rows)

    def put(lhs, index, value, right=False):
        each = value.shape[1]
        group = ROWS // each
        count = LAYERS * each
        for layer in range(0, LAYERS, group):
            block = jnp.concatenate([value[layer + at] for at in range(group)], 0) if group > 1 else value[layer]
            for at, part in enumerate(split3(block)):
                begin = (3 * index + at) * count + layer * each
                if right:
                    lhs[begin : begin + ROWS, LANES:] = part
                else:
                    lhs[begin : begin + ROWS, :LANES] = part

    def multiply(lhs, result, block, index=None):
        each = lhs.shape[0] // 2
        span = slice(0, 2 * each) if index is None else slice(index * each, (index + 1) * each)
        result[span] = jnp.dot(lhs[span], mats[block], preferred_element_type=F32)

    def column(result, index, layer):
        per = result.shape[0] // 6
        count = per // LAYERS
        begin = 3 * index * per + layer * count
        part = lambda at: result[begin + at * per : begin + at * per + count]
        return (part(0) + part(1)) + part(2)

    def fill(ext, own, beside, layer):
        ext[layer, pl.ds(pl.multiple_of(24 * after, 8), 8), :] = beside
        if rows == ROWS:
            ext[layer, 8:24, :] = own[layer]
        else:
            begin = pl.multiple_of(8 * after, 8)
            ext[layer, pl.ds(begin + 8, 8), :] = own[layer, pl.ds(begin, 8), :]

    def load_ext(slot, one, two, source):
        for layer in range(LAYERS):
            beside = source[layer]
            fill(ext_refs.at[slot, 0], one, beside, layer)
            fill(ext_refs.at[slot, 1], two, sroll(beside, 4), layer)
        for k in (0, 1):
            put(lhs_f.at[slot], k, ext_refs[slot, k, :, main, :])

    for layer in range(LAYERS):
        beside = message[1][2, layer]
        fill(h_ext.at[0], hm.at[0], beside, layer)
        fill(h_ext.at[1], hm.at[1], sroll(beside, 4), layer)
        fill(w_ext, w, message[1][1, layer], layer)
    for k in (0, 1):
        put(lhs_f.at[0], k, h_ext[k, :, main, :], True)
    load_ext(0, m1, m2, message[1].at[0])
    multiply(lhs_f.at[0], res_f.at[0], dirs, 0)
    multiply(lhs_f.at[0], res_f.at[0], dirs + 1, 1)
    for slot in range(1, slots):
        for k in (0, 1):
            put(lhs_f.at[slot], k, h_ext[k, :, main, :], True)

    def slopes(slot, k, layer, layers):
        return (
            diff_x(ext_refs.at[slot, k], layer, start, rows),
            column(res_f.at[slot], k, layer),
            diff_z(layers, layer),
        )

    def loaded(slot):
        return tuple(layers_of(ext_refs.at[slot, k], start, rows) for k in (0, 1))

    fold = -1.0 / 20736.0
    block = lane((rows, LANES)) // 8
    within = lane((rows, LANES)) % 8

    def spread(value, at):
        return jnp.take_along_axis(value, within + 8 * at, axis=1)

    packed = tuple(layers_of(h_ext.at[k], start, rows) for k in (0, 1))
    for layer in range(LAYERS):
        first, second = (
            (
                diff_x(h_ext.at[k], layer, start, rows),
                hy[k, layer, main, :],
                diff_z(packed[k], layer),
            )
            for k in (0, 1)
        )
        one = tuple(spread(part, dirs) for part in first)
        two = tuple(spread(part, dirs + 1) for part in second)
        weight = spread(h_ext[0, layer, main, :], dirs + 1) * fold
        second = tuple(jnp.where(block == dirs, 0.0, part) for part in second)
        left_term = cross(first, two)
        right_term = cross(one, second)
        rw = tuple(weight * (left_term[i] + right_term[i]) for i in range(3))
        cor[0, layer, :rows, :] = cross(two, rw)[1]
        cor[1, layer, :rows, :] = cross(rw, one)[1]
    for slot in range(slots):
        for k in (0, 1):
            put(lhs_a.at[slot], k, cor[k, :, 2 : 2 + wide, :], True)

    models = loaded(0)
    for layer in range(LAYERS):
        for k, ref in ((0, s1), (1, s2)):
            for index, part in enumerate(slopes(0, k, layer, models[k])):
                ref[index, layer] = part

    def products(slot, second_field):
        held = loaded(slot)
        for layer in range(LAYERS):
            one = (s1[0, layer], s1[1, layer], s1[2, layer])
            two = (s2[0, layer], s2[1, layer], s2[2, layer])
            if second_field:
                perturbed = tuple(
                    p + q
                    for p, q in zip(
                        cross(slopes(slot, 0, layer, held[0]), two), cross(one, slopes(slot, 1, layer, held[1]))
                    )
                )
            else:
                perturbed = cross(one, two)
            weight = w_ext[layer, main, :] * fold
            rw = tuple(weight * part for part in perturbed)
            for k, adj in ((0, cross(two, rw)), (1, cross(rw, one))):
                ax[slot, k, layer, :rows, :] = adj[0]
                ay[slot, k, layer, :rows, :] = adj[1]
                az[slot, k, layer, :rows, :] = adj[2]
        for k in (0, 1):
            put(lhs_a.at[slot], k, ay[slot, k, :, 2 : 2 + wide, :])

    def divergence(slot, targets):
        for k in (0, 1):
            layers = layers_of(az.at[slot, k], 2, wide)
            for layer in range(LAYERS):
                total = (
                    diff_x(ax.at[slot, k], layer, 2, wide)
                    + column(res_a.at[slot], k, layer)
                    + diff_z(layers, layer)
                )
                targets[k][layer, pl.ds(first_row + 2, rows - 4), :] = total[: rows - 4]

    g1, g2, h1, h2 = outs
    products(0, False)
    multiply(lhs_a.at[0], res_a.at[0], dirs)
    divergence(0, (g1, g2))
    done(None)

    def batch(begin, count):
        for slot in range(count):
            load_ext(slot, d1.at[begin + slot], d2.at[begin + slot], message[0].at[begin + slot])
            multiply(lhs_f.at[slot], res_f.at[slot], begin + slot)
        for slot in range(count):
            products(slot, True)
            multiply(lhs_a.at[slot], res_a.at[slot], begin + slot)
        for slot in range(count):
            divergence(slot, (h1.at[begin + slot], h2.at[begin + slot]))
            done(begin + slot)

    @pl.loop(0, dirs // slots)
    def _(step):
        batch(step * slots, slots)

    if dirs % slots:
        batch(dirs - dirs % slots, dirs % slots)


def phase_scratch(rows, wide, slots):
    ext = scratch(LAYERS, EXT, LANES)
    slopes = scratch(3, LAYERS, rows, LANES)
    adjoint = scratch(slots, 2, LAYERS, rows + 16, LANES)
    return [
        scratch(slots, 2, LAYERS, EXT, LANES), scratch(2, LAYERS, EXT, LANES), ext, slopes, slopes,
        scratch(2, LAYERS, rows + 16, LANES), adjoint, adjoint, adjoint,
        half(slots, 6 * LAYERS * rows, 2 * LANES), half(slots, 6 * LAYERS * wide, 2 * LANES),
        scratch(slots, 6 * LAYERS * rows, LANES), scratch(slots, 6 * LAYERS * wide, LANES),
    ]


def halo_body(e1, e2, ya, yb, hy):
    low = (lane((ROWS, LANES)) % 8) < 4
    for layer in range(LAYERS):
        left, right, left2, right2 = sides(ya, yb, layer)
        for k, own, before, after in ((0, e1[layer], left, right), (1, e2[layer], left2, right2)):
            before = diff_y(jnp.where(low, before, own))
            after = diff_y(jnp.where(low, own, after))
            hy[k, layer, 8:24, :] = jnp.where(low, before, after)
            hy[k, layer, 0:8, :] = jnp.zeros((8, LANES), F32)
            hy[k, layer, 24:32, :] = jnp.zeros((8, LANES), F32)


def near_body(dirs, mats, fields, xa, xa_rest, hm, hy, g1, g2, h1, h2, *refs):
    core = lax.rem(lax.axis_index("gx"), 2)
    phase(
        dirs, 16, 16, NEAR_SLOTS, 2 - 4 * core, 1 - core, mats, fields, (xa, xa_rest), hm, hy, (g1, g2, h1, h2), lambda d: None, refs
    )


def rest_body(
    dirs, mats, fields, xb, hm, hy, g1_in, g2_in, h1_in, h2_in,
    g1_out, g2_out, h1_out, h2_out, g1, g2, h1, h2, sems, *refs,
):
    core = lax.rem(lax.axis_index("gx"), 2)

    def copies(d):
        if d is None:
            return (
                pltpu.make_async_copy(g1, g1_out, sems.at[0, dirs]),
                pltpu.make_async_copy(g2, g2_out, sems.at[1, dirs]),
            )
        return (
            pltpu.make_async_copy(h1.at[d], h1_out.at[d], sems.at[0, d]),
            pltpu.make_async_copy(h2.at[d], h2_out.at[d], sems.at[1, d]),
        )

    def done(d):
        for copy in copies(d):
            copy.start()

    g1[...] = g1_in[...]
    g2[...] = g2_in[...]
    h1[...] = h1_in[...]
    h2[...] = h2_in[...]
    phase(dirs, 8, 8, REST_SLOTS, 12 * core - 2, core, mats, fields, (xb, xb.at[pl.ds(dirs, 3)]), hm, hy, (g1, g2, h1, h2), done, refs)

    @pl.loop(0, dirs)
    def _(d):
        for copy in copies(d):
            copy.wait()

    for copy in copies(None):
        copy.wait()


def params():
    return pltpu.CompilerParams(vmem_limit_bytes=40 * MIB)


def cost(mib):
    return pl.CostEstimate(flops=0, bytes_accessed=mib * MIB, transcendentals=0)


def shards(model_one, model_two, weight, direction_one, direction_two):
    dirs = direction_one.shape[0]
    tile = shape(LAYERS, ROWS, LANES)
    many = shape(dirs, LAYERS, ROWS, LANES)
    message = shape(dirs + 3, LAYERS, 8, LANES)
    many_rows, few_rows = shape(dirs, LAYERS, 8, LANES), shape(3, LAYERS, 8, LANES)
    tile_s = scratch(LAYERS, ROWS, LANES)
    many_s = scratch(dirs, LAYERS, ROWS, LANES)
    fields = jnp.concatenate(
        [direction_one, model_one[None], direction_two, model_two[None], weight[None]], 0
    )
    count_x, count_y = lax.axis_size("gx"), lax.axis_size("gy")
    mats = pl.pallas_call(
        setup_body,
        out_shape=jax.ShapeDtypeStruct((dirs + 2, 2 * LANES, LANES), jnp.bfloat16),
        cost_estimate=cost(64),
        compiler_params=params(),
        name="setup",
    )()
    e1, e2, ya, yb = pl.pallas_call(
        functools.partial(pack_body, dirs),
        out_shape=(tile,) * 4,
        compiler_params=params(),
        name="pack",
    )(fields)
    yb = lax.ppermute(yb, "gy", swap(count_y, 1))
    ya = lax.ppermute(ya, "gy", swap(count_y, 0))
    xb, hm = pl.pallas_call(
        functools.partial(rows_body, dirs),
        out_shape=(message, shape(2, LAYERS, ROWS, LANES)),
        compiler_params=params(),
        name="rows",
    )(ya, yb, fields)
    xb = lax.ppermute(xb, "gx", swap(count_x, 1))
    xa, xa_rest = pl.pallas_call(
        functools.partial(core_body, dirs),
        out_shape=(many_rows, few_rows),
        cost_estimate=cost(4),
        compiler_params=params(),
        name="core",
    )(fields, hm)
    xa = lax.ppermute(xa, "gx", swap(count_x, 0))
    xa_rest = lax.ppermute(xa_rest, "gx", swap(count_x, 0))
    hy = pl.pallas_call(
        halo_body,
        out_shape=shape(2, LAYERS, EXT, LANES),
        cost_estimate=cost(2),
        compiler_params=params(),
        name="halo",
    )(e1, e2, ya, yb)
    g1, g2, h1, h2 = pl.pallas_call(
        functools.partial(near_body, dirs),
        out_shape=(tile, tile, many, many),
        scratch_shapes=phase_scratch(16, 16, NEAR_SLOTS),
        cost_estimate=cost(16),
        compiler_params=params(),
        name="near",
    )(mats, fields, xa, xa_rest, hm, hy)
    return pl.pallas_call(
        functools.partial(rest_body, dirs),
        out_shape=(tile, tile, many, many),
        out_specs=[pl.BlockSpec(memory_space=pltpu.HBM)] * 4,
        scratch_shapes=[tile_s, tile_s, many_s, many_s, pltpu.SemaphoreType.DMA((2, dirs + 1))] + phase_scratch(8, 8, REST_SLOTS),
        cost_estimate=cost(8),
        compiler_params=params(),
        name="rest",
    )(mats, fields, xb, hm, hy, g1, g2, h1, h2)


def solution(mesh):
    plane = P(None, "gx", "gy")
    stack = P(None, None, "gx", "gy")
    return jax.shard_map(
        shards,
        mesh=mesh,
        in_specs=(plane, plane, plane, stack, stack),
        out_specs=(plane, plane, stack, stack),
        check_vma=False,
    )
```

```python
import functools

import jax
import jax.numpy as jnp
from jax import lax
from jax.experimental import pallas as pl
from jax.experimental.pallas import tpu as pltpu
from jax.sharding import PartitionSpec as P

LAYERS = 8
ROWS = 16
EXT = 32
LANES = 128
MIB = 1024 * 1024
NEAR_SLOTS = 5
REST_SLOTS = 10
F32 = jnp.float32


def swap(count, first):
    pairs = []
    for low in range(first, count - 1, 2):
        pairs += [(low, low + 1), (low + 1, low)]
    return pairs


def shape(*dims):
    return jax.ShapeDtypeStruct(dims, F32)


def scratch(*dims):
    return pltpu.VMEM(dims, F32)


def half(*dims):
    return pltpu.VMEM(dims, jnp.bfloat16)


def lane(dims):
    return lax.broadcasted_iota(jnp.int32, dims, len(dims) - 1)


def sub(dims):
    return lax.broadcasted_iota(jnp.int32, dims, len(dims) - 2)


def lroll(value, amount):
    return pltpu.roll(value, amount % LANES, axis=value.ndim - 1)


def sroll(value, amount):
    return pltpu.roll(value, amount % value.shape[-2], axis=value.ndim - 2)


def split(dirs, fields):
    return (
        fields.at[2 * dirs],
        fields.at[2 * dirs + 1],
        fields.at[2 * dirs + 2],
        fields.at[pl.ds(0, dirs)],
        fields.at[pl.ds(dirs, dirs)],
    )


def pack_body(dirs, fields, e1, e2, ya, yb):
    m1, m2, w, d1, d2 = split(dirs, fields)
    side = lax.rem(lax.axis_index("gy"), 2)
    block = lane((ROWS, LANES)) // 8
    low = (lane((ROWS, LANES)) % 8) < 4
    for layer in range(LAYERS):
        one = jnp.zeros((ROWS, LANES), F32)
        two = jnp.zeros((ROWS, LANES), F32)
        for d in range(dirs):
            one = jnp.where(block == d, lroll(d1[d, layer], 8 * d + 4), one)
            two = jnp.where(block == d, lroll(d2[d, layer], 8 * d + 4), two)
        one = jnp.where(block == dirs, lroll(m1[layer], 8 * dirs + 4), one)
        one = jnp.where(block == dirs + 1, lroll(w[layer], 8 * dirs + 12), one)
        two = jnp.where(block == dirs + 1, lroll(m2[layer], 8 * dirs + 12), two)
        e1[layer] = one
        e2[layer] = two
        tail = jnp.where(low, one, lroll(two, 4))
        head = jnp.where(low, lroll(two, -4), one)
        ya[layer] = jnp.where(side == 0, tail, head)
        yb[layer] = jnp.where(side == 0, head, tail)


def edge_rows(one, two, tail, layer):
    upper = (sub((8, LANES)) >= 4).astype(jnp.int32)
    start = pl.multiple_of(tail * 8, 8)
    first = one[layer, pl.ds(start, 8), :]
    second = two[layer, pl.ds(start, 8), :]
    return jnp.where(upper == tail, first, sroll(second, 4))


def sides(ya, yb, layer):
    side = lax.rem(lax.axis_index("gy"), 2)
    from_a, from_b = ya[layer], yb[layer]
    left = jnp.where(side == 0, from_b, from_a)
    right = jnp.where(side == 0, from_a, from_b)
    return left, right, lroll(left, -4), lroll(right, 4)


def rows_body(dirs, ya, yb, fields, xb, hm):
    low = (lane((ROWS, LANES)) % 8) < 4
    for layer in range(LAYERS):
        left, right, left2, right2 = sides(ya, yb, layer)
        hm[0, layer] = jnp.where(low, left, right)
        hm[1, layer] = jnp.where(low, left2, right2)
    message_rows(dirs, lax.rem(lax.axis_index("gx"), 2), fields, hm, (xb, xb.at[pl.ds(dirs, 3)]))


def message_rows(dirs, tail, fields, hm, out):
    m1, m2, w, d1, d2 = split(dirs, fields)
    pairs = [(d1.at[d], d2.at[d]) for d in range(dirs)] + [(m1, m2), (w, w), (hm.at[0], hm.at[1])]
    for index, (one, two) in enumerate(pairs):
        for layer in range(LAYERS):
            target = out[0].at[index] if index < dirs else out[1].at[index - dirs]
            target[layer] = edge_rows(one, two, tail, layer)


def core_body(dirs, fields, hm, xa, xa_rest):
    message_rows(dirs, 1 - lax.rem(lax.axis_index("gx"), 2), fields, hm, (xa, xa_rest))


def stencil(up2, up1, down1, down2):
    return 8.0 * (up1 - down1) - (up2 - down2)


def diff_x(ref, layer, start, rows):
    at = lambda offset: ref[layer, pl.ds(start + offset, rows), :]
    return stencil(at(2), at(1), at(-1), at(-2))


def diff_y(value):
    return stencil(lroll(value, -2), lroll(value, -1), lroll(value, 1), lroll(value, 2))


def layers_of(ref, start, rows):
    held = {}

    def at(layer):
        if not 0 <= layer < LAYERS:
            return None
        if layer not in held:
            held[layer] = ref[layer, pl.ds(start, rows), :]
        return held[layer]

    return at


def diff_z(at, layer):
    up2, up1, down1, down2 = at(layer + 2), at(layer + 1), at(layer - 1), at(layer - 2)
    if up1 is None:
        total = -8.0 * down1
    elif down1 is None:
        total = 8.0 * up1
    else:
        total = 8.0 * (up1 - down1)
    if up2 is not None:
        total = total - up2
    if down2 is not None:
        total = total + down2
    return total


def cross(left, right):
    return (
        left[1] * right[2] - left[2] * right[1],
        left[2] * right[0] - left[0] * right[2],
        left[0] * right[1] - left[1] * right[0],
    )


def split3(value):
    high = value.astype(jnp.bfloat16)
    rest = value - high.astype(F32)
    mid = rest.astype(jnp.bfloat16)
    return high, mid, (rest - mid.astype(F32)).astype(jnp.bfloat16)


def band():
    gap = lax.broadcasted_iota(jnp.int32, (LANES, LANES), 0) - lax.broadcasted_iota(jnp.int32, (LANES, LANES), 1)
    near = jnp.where(gap == 1, 8.0, jnp.where(gap == -1, -8.0, 0.0))
    far = jnp.where(gap == 2, -1.0, jnp.where(gap == -2, 1.0, 0.0))
    return (near + far).astype(jnp.bfloat16)


def edge_rows_matrix(block):
    row = lax.broadcasted_iota(jnp.int32, (16, LANES), 0) - 8 * (block % 2)
    col = lax.broadcasted_iota(jnp.int32, (16, LANES), 1)
    table = jnp.zeros((16, LANES), F32)
    for k, c, factor in ((2, 0, 1.0), (3, 0, -8.0), (3, 1, 1.0), (4, 126, -1.0), (4, 127, 8.0), (5, 127, -1.0)):
        table = jnp.where((row == k) & (col == c), factor, table)
    return table.astype(jnp.bfloat16)


def setup_body(mats):
    mats[...] = jnp.zeros(mats.shape, jnp.bfloat16)
    for block in range(mats.shape[0]):
        mats[block, :LANES, :] = band()
        start = LANES + 16 * (block // 2)
        mats[block, start : start + 16, :] = edge_rows_matrix(block)


def phase(dirs, rows, wide, slots, first_row, after, mats, fields, message, hm, hy, outs, done, refs):
    m1, m2, w, d1, d2 = split(dirs, fields)
    ext_refs, h_ext, w_ext, s1, s2, cor, ax, ay, az, lhs_f, lhs_a, res_f, res_a = refs
    start = first_row + 8
    main = pl.ds(start, rows)

    def put(lhs, index, value, right=False):
        each = value.shape[1]
        group = ROWS // each
        count = LAYERS * each
        for layer in range(0, LAYERS, group):
            block = jnp.concatenate([value[layer + at] for at in range(group)], 0) if group > 1 else value[layer]
            for at, part in enumerate(split3(block)):
                begin = (3 * index + at) * count + layer * each
                if right:
                    lhs[begin : begin + ROWS, LANES:] = part
                else:
                    lhs[begin : begin + ROWS, :LANES] = part

    def multiply(lhs, result, block, index=None):
        each = lhs.shape[0] // 2
        span = slice(0, 2 * each) if index is None else slice(index * each, (index + 1) * each)
        result[span] = jnp.dot(lhs[span], mats[block], preferred_element_type=F32)

    def column(result, index, layer):
        per = result.shape[0] // 6
        count = per // LAYERS
        begin = 3 * index * per + layer * count
        part = lambda at: result[begin + at * per : begin + at * per + count]
        return (part(0) + part(1)) + part(2)

    def fill(ext, own, beside, layer):
        ext[layer, pl.ds(pl.multiple_of(24 * after, 8), 8), :] = beside
        if rows == ROWS:
            ext[layer, 8:24, :] = own[layer]
        else:
            begin = pl.multiple_of(8 * after, 8)
            ext[layer, pl.ds(begin + 8, 8), :] = own[layer, pl.ds(begin, 8), :]

    def load_ext(slot, one, two, source):
        for layer in range(LAYERS):
            beside = source[layer]
            fill(ext_refs.at[slot, 0], one, beside, layer)
            fill(ext_refs.at[slot, 1], two, sroll(beside, 4), layer)
        for k in (0, 1):
            put(lhs_f.at[slot], k, ext_refs[slot, k, :, main, :])

    for layer in range(LAYERS):
        beside = message[1][2, layer]
        fill(h_ext.at[0], hm.at[0], beside, layer)
        fill(h_ext.at[1], hm.at[1], sroll(beside, 4), layer)
        fill(w_ext, w, message[1][1, layer], layer)
    for k in (0, 1):
        put(lhs_f.at[0], k, h_ext[k, :, main, :], True)
    load_ext(0, m1, m2, message[1].at[0])
    multiply(lhs_f.at[0], res_f.at[0], dirs, 0)
    multiply(lhs_f.at[0], res_f.at[0], dirs + 1, 1)
    for slot in range(1, slots):
        for k in (0, 1):
            put(lhs_f.at[slot], k, h_ext[k, :, main, :], True)

    def slopes(slot, k, layer, layers):
        return (
            diff_x(ext_refs.at[slot, k], layer, start, rows),
            column(res_f.at[slot], k, layer),
            diff_z(layers, layer),
        )

    def loaded(slot):
        return tuple(layers_of(ext_refs.at[slot, k], start, rows) for k in (0, 1))

    fold = -1.0 / 20736.0
    block = lane((rows, LANES)) // 8
    within = lane((rows, LANES)) % 8

    def spread(value, at):
        return jnp.take_along_axis(value, within + 8 * at, axis=1)

    packed = tuple(layers_of(h_ext.at[k], start, rows) for k in (0, 1))
    for layer in range(LAYERS):
        first, second = (
            (
                diff_x(h_ext.at[k], layer, start, rows),
                hy[k, layer, main, :],
                diff_z(packed[k], layer),
            )
            for k in (0, 1)
        )
        one = tuple(spread(part, dirs) for part in first)
        two = tuple(spread(part, dirs + 1) for part in second)
        weight = spread(h_ext[0, layer, main, :], dirs + 1) * fold
        second = tuple(jnp.where(block == dirs, 0.0, part) for part in second)
        left_term = cross(first, two)
        right_term = cross(one, second)
        rw = tuple(weight * (left_term[i] + right_term[i]) for i in range(3))
        cor[0, layer, :rows, :] = cross(two, rw)[1]
        cor[1, layer, :rows, :] = cross(rw, one)[1]
    for slot in range(slots):
        for k in (0, 1):
            put(lhs_a.at[slot], k, cor[k, :, 2 : 2 + wide, :], True)

    models = loaded(0)
    for layer in range(LAYERS):
        for k, ref in ((0, s1), (1, s2)):
            for index, part in enumerate(slopes(0, k, layer, models[k])):
                ref[index, layer] = part

    def products(slot, second_field):
        held = loaded(slot)
        for layer in range(LAYERS):
            one = (s1[0, layer], s1[1, layer], s1[2, layer])
            two = (s2[0, layer], s2[1, layer], s2[2, layer])
            if second_field:
                perturbed = tuple(
                    p + q
                    for p, q in zip(
                        cross(slopes(slot, 0, layer, held[0]), two), cross(one, slopes(slot, 1, layer, held[1]))
                    )
                )
            else:
                perturbed = cross(one, two)
            weight = w_ext[layer, main, :] * fold
            rw = tuple(weight * part for part in perturbed)
            for k, adj in ((0, cross(two, rw)), (1, cross(rw, one))):
                ax[slot, k, layer, :rows, :] = adj[0]
                ay[slot, k, layer, :rows, :] = adj[1]
                az[slot, k, layer, :rows, :] = adj[2]
        for k in (0, 1):
            put(lhs_a.at[slot], k, ay[slot, k, :, 2 : 2 + wide, :])

    def divergence(slot, targets):
        for k in (0, 1):
            layers = layers_of(az.at[slot, k], 2, wide)
            for layer in range(LAYERS):
                total = (
                    diff_x(ax.at[slot, k], layer, 2, wide)
                    + column(res_a.at[slot], k, layer)
                    + diff_z(layers, layer)
                )
                targets[k][layer, pl.ds(first_row + 2, rows - 4), :] = total[: rows - 4]

    g1, g2, h1, h2 = outs
    products(0, False)
    multiply(lhs_a.at[0], res_a.at[0], dirs)
    divergence(0, (g1, g2))
    done(None)

    def batch(begin, count):
        for slot in range(count):
            load_ext(slot, d1.at[begin + slot], d2.at[begin + slot], message[0].at[begin + slot])
            multiply(lhs_f.at[slot], res_f.at[slot], begin + slot)
        for slot in range(count):
            products(slot, True)
            multiply(lhs_a.at[slot], res_a.at[slot], begin + slot)
        for slot in range(count):
            divergence(slot, (h1.at[begin + slot], h2.at[begin + slot]))
            done(begin + slot)

    @pl.loop(0, dirs // slots)
    def _(step):
        batch(step * slots, slots)

    if dirs % slots:
        batch(dirs - dirs % slots, dirs % slots)


def phase_scratch(rows, wide, slots):
    ext = scratch(LAYERS, EXT, LANES)
    slopes = scratch(3, LAYERS, rows, LANES)
    adjoint = scratch(slots, 2, LAYERS, rows + 16, LANES)
    return [
        scratch(slots, 2, LAYERS, EXT, LANES), scratch(2, LAYERS, EXT, LANES), ext, slopes, slopes,
        scratch(2, LAYERS, rows + 16, LANES), adjoint, adjoint, adjoint,
        half(slots, 6 * LAYERS * rows, 2 * LANES), half(slots, 6 * LAYERS * wide, 2 * LANES),
        scratch(slots, 6 * LAYERS * rows, LANES), scratch(slots, 6 * LAYERS * wide, LANES),
    ]


def halo_body(e1, e2, ya, yb, hy):
    low = (lane((ROWS, LANES)) % 8) < 4
    for layer in range(LAYERS):
        left, right, left2, right2 = sides(ya, yb, layer)
        for k, own, before, after in ((0, e1[layer], left, right), (1, e2[layer], left2, right2)):
            before = diff_y(jnp.where(low, before, own))
            after = diff_y(jnp.where(low, own, after))
            hy[k, layer, 8:24, :] = jnp.where(low, before, after)
            hy[k, layer, 0:8, :] = jnp.zeros((8, LANES), F32)
            hy[k, layer, 24:32, :] = jnp.zeros((8, LANES), F32)


def near_body(dirs, mats, fields, xa, xa_rest, hm, hy, g1, g2, h1, h2, *refs):
    core = lax.rem(lax.axis_index("gx"), 2)
    phase(
        dirs, 16, 16, NEAR_SLOTS, 2 - 4 * core, 1 - core, mats, fields, (xa, xa_rest), hm, hy, (g1, g2, h1, h2), lambda d: None, refs
    )


def rest_body(
    dirs, mats, fields, xb, hm, hy, g1_in, g2_in, h1_in, h2_in,
    g1_out, g2_out, h1_out, h2_out, g1, g2, h1, h2, sems, *refs,
):
    core = lax.rem(lax.axis_index("gx"), 2)

    def copies(d):
        if d is None:
            return (
                pltpu.make_async_copy(g1, g1_out, sems.at[0, dirs]),
                pltpu.make_async_copy(g2, g2_out, sems.at[1, dirs]),
            )
        return (
            pltpu.make_async_copy(h1.at[d], h1_out.at[d], sems.at[0, d]),
            pltpu.make_async_copy(h2.at[d], h2_out.at[d], sems.at[1, d]),
        )

    def done(d):
        for copy in copies(d):
            copy.start()

    g1[...] = g1_in[...]
    g2[...] = g2_in[...]
    h1[...] = h1_in[...]
    h2[...] = h2_in[...]
    phase(dirs, 8, 8, REST_SLOTS, 12 * core - 2, core, mats, fields, (xb, xb.at[pl.ds(dirs, 3)]), hm, hy, (g1, g2, h1, h2), done, refs)

    @pl.loop(0, dirs)
    def _(d):
        for copy in copies(d):
            copy.wait()

    for copy in copies(None):
        copy.wait()


def params():
    return pltpu.CompilerParams(vmem_limit_bytes=40 * MIB)


def cost(mib):
    return pl.CostEstimate(flops=0, bytes_accessed=mib * MIB, transcendentals=0)


def shards(model_one, model_two, weight, direction_one, direction_two):
    dirs = direction_one.shape[0]
    tile = shape(LAYERS, ROWS, LANES)
    many = shape(dirs, LAYERS, ROWS, LANES)
    message = shape(dirs + 3, LAYERS, 8, LANES)
    many_rows, few_rows = shape(dirs, LAYERS, 8, LANES), shape(3, LAYERS, 8, LANES)
    tile_s = scratch(LAYERS, ROWS, LANES)
    many_s = scratch(dirs, LAYERS, ROWS, LANES)
    fields = jnp.concatenate(
        [direction_one, direction_two, model_one[None], model_two[None], weight[None]], 0
    )
    count_x, count_y = lax.axis_size("gx"), lax.axis_size("gy")
    mats = pl.pallas_call(
        setup_body,
        out_shape=jax.ShapeDtypeStruct((dirs + 2, 2 * LANES, LANES), jnp.bfloat16),
        cost_estimate=cost(64),
        compiler_params=params(),
        name="setup",
    )()
    e1, e2, ya, yb = pl.pallas_call(
        functools.partial(pack_body, dirs),
        out_shape=(tile,) * 4,
        compiler_params=params(),
        name="pack",
    )(fields)
    yb = lax.ppermute(yb, "gy", swap(count_y, 1))
    ya = lax.ppermute(ya, "gy", swap(count_y, 0))
    xb, hm = pl.pallas_call(
        functools.partial(rows_body, dirs),
        out_shape=(message, shape(2, LAYERS, ROWS, LANES)),
        compiler_params=params(),
        name="rows",
    )(ya, yb, fields)
    xb = lax.ppermute(xb, "gx", swap(count_x, 1))
    xa, xa_rest = pl.pallas_call(
        functools.partial(core_body, dirs),
        out_shape=(many_rows, few_rows),
        cost_estimate=cost(4),
        compiler_params=params(),
        name="core",
    )(fields, hm)
    xa = lax.ppermute(xa, "gx", swap(count_x, 0))
    xa_rest = lax.ppermute(xa_rest, "gx", swap(count_x, 0))
    hy = pl.pallas_call(
        halo_body,
        out_shape=shape(2, LAYERS, EXT, LANES),
        cost_estimate=cost(2),
        compiler_params=params(),
        name="halo",
    )(e1, e2, ya, yb)
    g1, g2, h1, h2 = pl.pallas_call(
        functools.partial(near_body, dirs),
        out_shape=(tile, tile, many, many),
        scratch_shapes=phase_scratch(16, 16, NEAR_SLOTS),
        cost_estimate=cost(16),
        compiler_params=params(),
        name="near",
    )(mats, fields, xa, xa_rest, hm, hy)
    return pl.pallas_call(
        functools.partial(rest_body, dirs),
        out_shape=(tile, tile, many, many),
        out_specs=[pl.BlockSpec(memory_space=pltpu.HBM)] * 4,
        scratch_shapes=[tile_s, tile_s, many_s, many_s, pltpu.SemaphoreType.DMA((2, dirs + 1))] + phase_scratch(8, 8, REST_SLOTS),
        cost_estimate=cost(8),
        compiler_params=params(),
        name="rest",
    )(mats, fields, xb, hm, hy, g1, g2, h1, h2)


def solution(mesh):
    plane = P(None, "gx", "gy")
    stack = P(None, None, "gx", "gy")
    return jax.shard_map(
        shards,
        mesh=mesh,
        in_specs=(plane, plane, plane, stack, stack),
        out_specs=(plane, plane, stack, stack),
        check_vma=False,
    )
```
